32 devices in a mesh: band: 2 (over x), grow: 4 (over z), gcol: 4 (over y, core).
Axes of the slice: x: 2, y: 2, z: 4, core: 2. Of those that a mesh axis runs over, the one named last changes fastest.
Arguments:
- valence: bfloat16 [4, 110592], replicated, may hold values from -6 to 6
- conduction: bfloat16 [32, 110592], P(('band', 'grow', 'gcol')), may hold values from -6 to 6
- val_energy: float32 [4], replicated, may hold values from -1 to 0
- cond_energy: float32 [32], replicated, may hold values from 0.2 to 3
- frequencies: float32 [2], replicated, may hold values from 0.1 to 2
- gvec_index: int32 [2048], replicated, may hold values from 0 to 110591, as said below
- first_band: int32 [4], replicated, may hold values from 0 to 15
Outputs:
- chi_zero: bfloat16 [2048, 2, 2, 2048], P(('grow', 'band'), None, None, 'gcol')
The draws below stay inside these ranges and needn't reach their ends.
Inputs may be any that keep to these rules, and one draw needn't show every extreme that they name: `gvec_index`: all 2048 entries are different.
All inputs are finite; a program needn't handle non-finite values.
Results may differ from the reference program's by a relative error of at most 0.0059.
Values may be sent and summed in bfloat16 or wider, within the bound.
A program may use at most 128 MiB of HBM per device.

```python
import math
import jax
import jax.numpy as jnp
from jax import lax

NV = 4
GRID = 48
NGV = 2048
NW = 2
NC = 32


def draw_gvec_index(key, part):
    key = jax.random.fold_in(key, 1)
    first_key, second_key = jax.random.split(key)
    total = GRID ** 3
    inner = jax.random.permutation(first_key, total - 2)[:NGV - 2].astype(jnp.int32) + 1
    whole = jnp.concatenate([jnp.zeros((1,), jnp.int32), inner, jnp.full((1,), total - 1, jnp.int32)])
    return whole[jax.random.permutation(second_key, NGV)]


def draw_first_band(key, part):
    key = jax.random.fold_in(key, 2)
    first_key, second_key = jax.random.split(key)
    values = jax.random.randint(first_key, (NV,), 0, NC // 2).astype(jnp.int32)
    values = values.at[0].set(0).at[1].set(NC // 2 - 1)
    return values[jax.random.permutation(second_key, NV)]


def block_scale(key, extent, shards, low, high):
    def one(dim, blocks):
        steps = jax.random.uniform(jax.random.fold_in(jax.random.fold_in(key, 6), dim), (blocks,), jnp.float32, low / len(shards), high / len(shards))
        return jnp.repeat(jnp.exp(steps), extent[dim] // blocks).reshape((-1,) + (1,) * (len(extent) - dim - 1))

    gain = one(*shards[0])
    for cut in shards[1:]:
        gain = gain * one(*cut)
    return gain


def scatter_about(key, shape, scale, limit, cuts=(), kind=jnp.bfloat16):
    result = jax.random.normal(key, shape, jnp.float32) * scale
    if len(cuts) > 0:
        result = block_scale(key, shape, cuts, -0.22, 0.18) * result
    return jnp.clip(result, min=-limit, max=limit).astype(kind)


def setup_inputs(seed: int = 0) -> dict:
    splits = jax.random.split(jax.random.key(seed), 8)
    return {
        "valence": scatter_about(splits[0], (NV, GRID ** 3), 1.0, 6.0),
        "conduction": scatter_about(splits[1], (NC, GRID ** 3), 1.0, 6.0, ((0, 32),)),
        "val_energy": jnp.clip(jax.random.uniform(splits[2], (NV,), jnp.float32, -1.0, 0.0), -1.0, 0.0),
        "cond_energy": jnp.clip(jax.random.uniform(splits[3], (NC,), jnp.float32, 0.2, 3.0), 0.2, 3.0),
        "frequencies": jnp.clip(jnp.exp(jax.random.uniform(splits[4], (NW,), jnp.float32, math.log(0.1), math.log(2.0))), 0.1, 2.0),
        "gvec_index": draw_gvec_index(jax.random.fold_in(splits[7], 71), 0),
        "first_band": draw_first_band(jax.random.fold_in(splits[7], 71), 0),
    }


def reference(valence, conduction, val_energy, cond_energy, frequencies, gvec_index, first_band):
    points = GRID ** 3
    block = math.gcd(NC, 16)
    val_float = valence.astype(jnp.float32)

    def dens_block(cond_block):
        pair = cond_block.astype(jnp.float32)[:, None, :] * val_float[None]
        cube = pair.reshape(block, NV, GRID, GRID, GRID)
        spectrum = jnp.fft.fftn(cube, axes=(2, 3, 4)).reshape(block, NV, points) * (GRID ** -1.5)
        picked = spectrum[:, :, gvec_index]
        return jnp.stack([jnp.real(picked), jnp.imag(picked)], 1).astype(jnp.bfloat16)

    density = lax.map(dens_block, conduction.reshape(NC // block, block, points))
    density = density.reshape(NC, 2, NV, NGV)
    gap_value = cond_energy[None, :] - val_energy[:, None]
    counted = jnp.arange(NC, dtype=jnp.int32)[None, :] >= first_band[:, None]
    weight = jnp.where(counted[None], -4.0 * gap_value[None] / (gap_value[None] ** 2 + frequencies[:, None, None] ** 2), 0.0) / (NV * NC)
    dens_float = density.astype(jnp.float32)
    right_main = dens_float.reshape(NC * 2 * NV, NGV)
    right_swap = jnp.stack([-dens_float[:, 1], dens_float[:, 0]], 1).reshape(NC * 2 * NV, NGV)
    results = []
    for freq in range(NW):
        left = (jnp.transpose(weight[freq])[:, None, :, None] * dens_float).astype(jnp.bfloat16)
        left_mat = left.astype(jnp.float32).reshape(NC * 2 * NV, NGV)
        real_part = jnp.dot(left_mat.T, right_main, precision=lax.Precision.HIGHEST)
        imag_part = jnp.dot(left_mat.T, right_swap, precision=lax.Precision.HIGHEST)
        results.append(jnp.stack([real_part, imag_part], 1))
    return jnp.stack(results, 1).astype(jnp.bfloat16)
```

```python
import functools
import math

import jax
import jax.numpy as jnp
import ml_dtypes
import numpy as np
from jax import lax
from jax.experimental import pallas as pl
from jax.experimental.pallas import tpu as pltpu
from jax.sharding import PartitionSpec as P

GRID = 48
HALF = GRID // 2 + 1
PLANE = GRID * GRID
CHUNK = 256
CHUNKS = -(-GRID * HALF // CHUNK)
TILE = 256
LANES = 128
MESH = pl.DeviceIdType.MESH
TABLE_SCALE = 1.622
TABLE_GAIN = 1.6242055647


def plane_table():
    line = np.arange(GRID)
    k2, k3 = np.meshgrid(line, np.arange(HALF), indexing="ij")
    k2, k3 = k2.reshape(-1), k3.reshape(-1)
    b, e = np.meshgrid(line, line, indexing="ij")
    b, e = b.reshape(-1), e.reshape(-1)
    turn = (b[:, None] * k2[None] + e[:, None] * k3[None]) % GRID
    angle = 2.0 * np.pi * line / GRID
    parts = []
    for values in (np.cos(angle), -np.sin(angle)):
        small = (values * TABLE_SCALE).astype(np.float32).astype(ml_dtypes.bfloat16)
        full = np.zeros((PLANE, CHUNKS * CHUNK), ml_dtypes.bfloat16)
        full[:, : GRID * HALF] = small[turn]
        parts.append(full.reshape(PLANE, CHUNKS, CHUNK).transpose(1, 0, 2))
    return np.concatenate(parts, 0)


def phase_table():
    line = np.arange(GRID)
    angle = 2.0 * np.pi * (line[:, None] * line[None] % GRID) / GRID
    scale = GRID ** (-1.5) / TABLE_GAIN
    both = np.zeros((2 * GRID, LANES), np.float32)
    both[:, :GRID] = np.concatenate([np.cos(angle), np.sin(angle)], 0) * scale
    high = both.astype(ml_dtypes.bfloat16)
    low = (both - high.astype(np.float32)).astype(ml_dtypes.bfloat16)
    return np.concatenate([high, low], 0)


def density_kernel(val_ref, cond_ref, table_ref, phase_ref, index_ref, out_ref, pair, planes):
    step = pl.program_id(0)
    rows = val_ref.shape[0]
    pairs = rows // GRID
    num_tiles = out_ref.shape[0]

    @pl.when(step == 0)
    def _():
        cond = cond_ref[...].astype(jnp.float32)
        for v in range(pairs):
            product = val_ref[v * GRID : (v + 1) * GRID].astype(jnp.float32) * cond
            high = product.astype(jnp.bfloat16)
            pair[v * GRID : (v + 1) * GRID] = high
            pair[rows + v * GRID : rows + (v + 1) * GRID] = (
                product - high.astype(jnp.float32)
            ).astype(jnp.bfloat16)

    both = jnp.dot(pair[...], table_ref[0], preferred_element_type=jnp.float32)
    plane = both[:rows] + both[rows:]
    high = plane.astype(jnp.bfloat16)
    planes[step, :rows] = high
    planes[step, rows:] = (plane - high.astype(jnp.float32)).astype(jnp.bfloat16)

    @pl.when(step == 2 * CHUNKS - 1)
    def _():
        @pl.loop(0, num_tiles)
        def _(tile):
            index = index_ref[tile]
            index_float = index.astype(jnp.float32)
            upper = jnp.floor((index_float + 0.5) * (1.0 / GRID))
            k3 = index_float - GRID * upper
            k1 = jnp.floor((upper + 0.5) * (1.0 / GRID))
            k2 = upper - GRID * k1
            mirror = k3 > HALF - 1
            k1 = jnp.where(mirror & (k1 > 0), GRID - k1, k1).astype(jnp.int32)
            k2 = jnp.where(mirror & (k2 > 0), GRID - k2, k2)
            k3 = jnp.where(mirror, GRID - k3, k3)
            sign = jnp.where(mirror, -1.0, 1.0)
            place = (k2 * HALF + k3).astype(jnp.int32)
            real = jnp.zeros((2 * rows, TILE), jnp.float32)
            imag = jnp.zeros((2 * rows, TILE), jnp.float32)
            line = lax.broadcasted_iota(jnp.int32, (CHUNK, TILE), 0)
            for chunk in range(CHUNKS):
                pick = jnp.where(line == place - chunk * CHUNK, 1.0, 0.0).astype(jnp.bfloat16)
                real += jnp.dot(planes[chunk], pick, preferred_element_type=jnp.float32)
                imag += jnp.dot(planes[CHUNKS + chunk], pick, preferred_element_type=jnp.float32)
            real = (real[:rows] + real[rows:]).reshape(pairs, GRID, TILE)
            imag = (imag[:rows] + imag[rows:]).reshape(pairs, GRID, TILE)
            pick = jnp.where(line[:LANES] == k1, 1.0, 0.0).astype(jnp.bfloat16)
            phases = jnp.dot(phase_ref[...], pick, preferred_element_type=jnp.float32)
            phases = phases[: 2 * GRID] + phases[2 * GRID :]
            cos_one, sin_one = phases[:GRID], phases[GRID:]
            out_real = jnp.sum(real * cos_one + imag * sin_one, axis=1)
            out_imag = jnp.sum(imag * cos_one - real * sin_one, axis=1) * sign
            out = jnp.concatenate([out_real, out_imag], 0)
            out = jnp.concatenate([out[:, :LANES], out[:, LANES:]], 0)
            out_ref[tile] = out.astype(jnp.bfloat16)


def tile_density(valence, conduction, gvec_index):
    val_count = valence.shape[0]
    rows = val_count * GRID
    num_tiles = gvec_index.shape[0] // TILE
    whole = lambda *shape: pl.BlockSpec(shape, lambda n: (0,) * len(shape))
    return pl.pallas_call(
        density_kernel,
        grid=(2 * CHUNKS,),
        out_shape=jax.ShapeDtypeStruct((num_tiles, 4 * val_count, LANES), jnp.bfloat16),
        in_specs=[
            whole(rows, PLANE),
            whole(GRID, PLANE),
            pl.BlockSpec((1, PLANE, CHUNK), lambda n: (n, 0, 0)),
            whole(4 * GRID, LANES),
            whole(num_tiles, 1, TILE),
        ],
        out_specs=whole(num_tiles, 4 * val_count, LANES),
        scratch_shapes=[
            pltpu.VMEM((2 * rows, PLANE), jnp.bfloat16),
            pltpu.VMEM((2 * CHUNKS, 2 * rows, CHUNK), jnp.bfloat16),
        ],
        compiler_params=pltpu.CompilerParams(vmem_limit_bytes=48 * 2**20),
    )(
        valence.reshape(rows, PLANE),
        conduction.reshape(GRID, PLANE),
        jnp.asarray(plane_table()),
        jnp.asarray(phase_table()),
        gvec_index.reshape(num_tiles, 1, TILE),
    )


def device_of(number, sizes):
    band_count, grow_count, gcol_count = sizes
    return number // (grow_count * gcol_count), number // gcol_count % grow_count, number % gcol_count


def exchange_kernel(sizes, tiles_ref, weight_ref, out_ref, rows_in, cols_in, send_sem, recv_sem, own_sem):
    band_count, grow_count, gcol_count = sizes
    devices = band_count * grow_count * gcol_count
    num_tiles = tiles_ref.shape[0]
    col_tiles = num_tiles // gcol_count
    me = (lax.axis_index("band") * grow_count + lax.axis_index("grow")) * gcol_count + lax.axis_index("gcol")

    def row_tile(place):
        return (place[1] * band_count + place[0]) * num_tiles // (grow_count * band_count)

    barrier = pltpu.get_barrier_semaphore()

    @pl.loop(1, devices)
    def _(offset):
        place = device_of(lax.rem(me + offset, devices), sizes)
        pl.semaphore_signal(barrier, inc=1, device_id=place, device_id_type=MESH)

    pl.semaphore_wait(barrier, devices - 1)

    @pl.loop(1, devices)
    def _(offset):
        place = device_of(lax.rem(me + offset, devices), sizes)
        pltpu.make_async_remote_copy(
            tiles_ref.at[row_tile(place)], rows_in.at[me], send_sem.at[0], recv_sem.at[0],
            device_id=place, device_id_type=MESH,
        ).start()
        pltpu.make_async_remote_copy(
            tiles_ref.at[pl.ds(place[2] * col_tiles, col_tiles)], cols_in.at[me], send_sem.at[1], recv_sem.at[1],
            device_id=place, device_id_type=MESH,
        ).start()

    here = device_of(me, sizes)
    pltpu.make_async_copy(tiles_ref.at[row_tile(here)], rows_in.at[me], recv_sem.at[0]).start()
    pltpu.make_async_copy(
        tiles_ref.at[pl.ds(here[2] * col_tiles, col_tiles)], cols_in.at[me], recv_sem.at[1]
    ).start()
    pltpu.make_async_copy(rows_in, rows_in, recv_sem.at[0]).wait()
    pltpu.make_async_copy(cols_in, cols_in, recv_sem.at[1]).wait()
    for held, sem in ((rows_in, 0), (cols_in, 1)):
        others = held.at[pl.ds(0, devices - 1)]
        pltpu.make_async_copy(others, others, send_sem.at[sem]).wait()

    cols = cols_in[...].astype(jnp.float32)
    half = cols.shape[2] // 2
    depth = devices * half
    right = jnp.concatenate(
        [cols[:, tile, side * half : (side + 1) * half].reshape(depth, LANES)
         for tile in range(col_tiles) for side in range(2)], 1
    ).astype(jnp.bfloat16)
    rows = rows_in[...].astype(jnp.float32)
    for side in range(2):
        part = rows[:, side * half : (side + 1) * half]
        for freq in range(out_ref.shape[0]):
            left = part * weight_ref[freq]
            swapped = jnp.concatenate([left[:, half // 2 :], -left[:, : half // 2]], 1)
            for kind, value in enumerate((left, swapped)):
                value = value.reshape(depth, LANES).astype(jnp.bfloat16)
                out_ref[freq, kind, side * LANES : (side + 1) * LANES] = lax.dot_general(
                    value, right, (((0,), (0,)), ((), ())), preferred_element_type=jnp.float32
                ).astype(jnp.bfloat16)


def on_device(sizes, valence, conduction, val_energy, cond_energy, frequencies, gvec_index, first_band):
    band_count, grow_count, gcol_count = sizes
    devices = band_count * grow_count * gcol_count
    bands = cond_energy.shape[0]
    val_count = val_energy.shape[0]
    freq_count = frequencies.shape[0]
    num_gvec = gvec_index.shape[0]
    tiles = tile_density(valence, conduction, gvec_index)
    num_tiles = tiles.shape[0]
    col_tiles = num_tiles // gcol_count
    gap_value = cond_energy[None, :] - val_energy[:, None]
    counted = jnp.arange(bands, dtype=jnp.int32)[None, :] >= first_band[:, None]
    weight = (
        jnp.where(
            counted[None],
            -4.0 * gap_value[None] / (gap_value[None] ** 2 + frequencies[:, None, None] ** 2),
            0.0,
        )
        / (bands * val_count)
    )
    weight = jnp.transpose(weight, (0, 2, 1))[:, :, None, :, None]
    weight = jnp.broadcast_to(weight, (freq_count, bands, 2, val_count, LANES))
    weight = weight.reshape(freq_count, bands, 2 * val_count, LANES)
    out = pl.pallas_call(
        functools.partial(exchange_kernel, sizes),
        out_shape=jax.ShapeDtypeStruct((freq_count, 2, TILE, num_gvec // gcol_count), jnp.bfloat16),
        in_specs=[pl.BlockSpec(memory_space=pltpu.VMEM)] * 2,
        out_specs=pl.BlockSpec(memory_space=pltpu.VMEM),
        scratch_shapes=[
            pltpu.VMEM((devices,) + tiles.shape[1:], jnp.bfloat16),
            pltpu.VMEM((devices, col_tiles) + tiles.shape[1:], jnp.bfloat16),
            pltpu.SemaphoreType.DMA((2,)),
            pltpu.SemaphoreType.DMA((2,)),
            pltpu.SemaphoreType.DMA,
        ],
        compiler_params=pltpu.CompilerParams(
            collective_id=0, has_side_effects=True, vmem_limit_bytes=48 * 2**20
        ),
    )(tiles, weight)
    out = jnp.transpose(out, (2, 0, 1, 3))
    row_count = num_gvec // (grow_count * band_count)
    if row_count < TILE:
        block = lax.axis_index("grow") * band_count + lax.axis_index("band")
        out = lax.dynamic_slice_in_dim(out, block * row_count % TILE, row_count, 0)
    return out


def solution(mesh):
    sizes = tuple(mesh.shape[name] for name in ("band", "grow", "gcol"))
    return jax.shard_map(
        functools.partial(on_device, sizes),
        mesh=mesh,
        in_specs=(P(), P(("band", "grow", "gcol"), None), P(), P(), P(), P(), P()),
        out_specs=P(("grow", "band"), None, None, "gcol"),
        check_vma=False,
    )
```

```python
import functools
import math

import jax
import jax.numpy as jnp
import ml_dtypes
import numpy as np
from jax import lax
from jax.experimental import pallas as pl
from jax.experimental.pallas import tpu as pltpu
from jax.sharding import PartitionSpec as P

GRID = 48
HALF = GRID // 2 + 1
PLANE = GRID * GRID
CHUNK = 256
CHUNKS = -(-GRID * HALF // CHUNK)
TILE = 256
LANES = 128
MESH = pl.DeviceIdType.MESH
TABLE_SCALE = 1.622
TABLE_GAIN = 1.6242055647


def plane_table():
    line = np.arange(GRID)
    k2, k3 = np.meshgrid(line, np.arange(HALF), indexing="ij")
    k2, k3 = k2.reshape(-1), k3.reshape(-1)
    b, e = np.meshgrid(line, line, indexing="ij")
    b, e = b.reshape(-1), e.reshape(-1)
    turn = (b[:, None] * k2[None] + e[:, None] * k3[None]) % GRID
    angle = 2.0 * np.pi * line / GRID
    parts = []
    for values in (np.cos(angle), -np.sin(angle)):
        small = (values * TABLE_SCALE).astype(np.float32).astype(ml_dtypes.bfloat16)
        full = np.zeros((PLANE, CHUNKS * CHUNK), ml_dtypes.bfloat16)
        full[:, : GRID * HALF] = small[turn]
        parts.append(full.reshape(PLANE, CHUNKS, CHUNK).transpose(1, 0, 2))
    return np.concatenate(parts, 0)


def phase_table(val_count):
    line = np.arange(GRID)
    angle = 2.0 * np.pi * (line[:, None] * line[None] % GRID) / GRID
    scale = GRID ** (-1.5) / TABLE_GAIN
    both = np.concatenate([np.cos(angle), np.sin(angle)], 0).astype(np.float64) * scale
    both = np.repeat(both, val_count, 0).astype(np.float32)
    high = both.astype(ml_dtypes.bfloat16)
    low = (both - high.astype(np.float32)).astype(ml_dtypes.bfloat16)
    table = np.zeros((both.shape[0], LANES), ml_dtypes.bfloat16)
    table[:, :GRID] = high
    table[:, LANES // 2 : LANES // 2 + GRID] = low
    return table


def kernel(
    sizes, val_ref, cond_ref, table_ref, phase_ref, index_ref, val_energy, cond_energy, frequencies, first_band,
    out_ref, pair, planes, tiles, from_line, rows_in, cols_in, line_send, line_recv, plane_send, plane_recv,
):
    band_count, grow_count, gcol_count = sizes
    plane_count = band_count * gcol_count
    devices = plane_count * grow_count
    step = pl.program_id(0)
    val_count = val_ref.shape[0]
    rows = val_count * GRID
    num_tiles = tiles.shape[0]
    col_tiles = num_tiles // gcol_count
    freq_count = out_ref.shape[0]
    band, grow, gcol = (lax.axis_index(name) for name in ("band", "grow", "gcol"))
    plane = band * gcol_count + gcol
    barrier = pltpu.get_barrier_semaphore()

    def line_peer(offset):
        return band, lax.rem(grow + offset, grow_count), gcol

    def plane_peer(offset):
        number = lax.rem(plane + offset, plane_count)
        return number // gcol_count, grow, number % gcol_count

    def number_of(place):
        return (place[0] * grow_count + place[1]) * gcol_count + place[2]

    def row_tile(place):
        return (place[1] * band_count + place[0]) * num_tiles // (grow_count * band_count)

    @pl.when(step == 0)
    def _():
        for offset in range(1, grow_count):
            pl.semaphore_signal(barrier, inc=1, device_id=line_peer(offset), device_id_type=MESH)

        @pl.loop(1, plane_count)
        def _(offset):
            pl.semaphore_signal(barrier, inc=1, device_id=plane_peer(offset), device_id_type=MESH)

        group = 16 // val_count

        @pl.loop(0, GRID // group)
        def _(block):
            products = []
            for member in range(group):
                where = pl.ds(pl.multiple_of((block * group + member) * PLANE, LANES), PLANE)
                products.append(
                    val_ref[:, where].astype(jnp.float32) * cond_ref[:, where].astype(jnp.float32)
                )
            product = jnp.concatenate(products, 0)
            high = product.astype(jnp.bfloat16)
            start = pl.multiple_of(block * 16, 16)
            pair[pl.ds(start, 16)] = high
            pair[pl.ds(rows + start, 16)] = (product - high.astype(jnp.float32)).astype(jnp.bfloat16)

    both = jnp.dot(pair[...], table_ref[0], preferred_element_type=jnp.float32)
    total = both[:rows] + both[rows:]
    high = total.astype(jnp.bfloat16)
    planes[step, :rows] = high
    planes[step, rows:] = (total - high.astype(jnp.float32)).astype(jnp.bfloat16)

    @pl.when(step == 2 * CHUNKS - 1)
    def _():
        pl.semaphore_wait(barrier, grow_count - 1 + plane_count - 1)

        @pl.loop(0, num_tiles)
        def _(tile):
            index = index_ref[tile]
            index_float = index.astype(jnp.float32)
            upper = jnp.floor((index_float + 0.5) * (1.0 / GRID))
            k3 = index_float - GRID * upper
            k1 = jnp.floor((upper + 0.5) * (1.0 / GRID))
            k2 = upper - GRID * k1
            mirror = k3 > HALF - 1
            k1 = jnp.where(mirror & (k1 > 0), GRID - k1, k1).astype(jnp.int32)
            k2 = jnp.where(mirror & (k2 > 0), GRID - k2, k2)
            k3 = jnp.where(mirror, GRID - k3, k3)
            sign = jnp.where(mirror, -1.0, 1.0)
            place = (k2 * HALF + k3).astype(jnp.int32)
            real = jnp.zeros((2 * rows, TILE), jnp.float32)
            imag = jnp.zeros((2 * rows, TILE), jnp.float32)
            line = lax.broadcasted_iota(jnp.int32, (CHUNK, TILE), 0)
            for chunk in range(CHUNKS):
                pick = jnp.where(line == place - chunk * CHUNK, 1.0, 0.0).astype(jnp.bfloat16)
                real += jnp.dot(planes[chunk], pick, preferred_element_type=jnp.float32)
                imag += jnp.dot(planes[CHUNKS + chunk], pick, preferred_element_type=jnp.float32)
            real = real[:rows] + real[rows:]
            imag = imag[:rows] + imag[rows:]
            line = line[:LANES]
            pick = jnp.where((line == k1) | (line == k1 + LANES // 2), 1.0, 0.0).astype(jnp.bfloat16)
            phases = jnp.dot(phase_ref[...], pick, preferred_element_type=jnp.float32)
            cos_one, sin_one = phases[:rows], phases[rows:]
            out = []
            for value, flip in (
                (real * cos_one + imag * sin_one, None),
                (imag * cos_one - real * sin_one, sign),
            ):
                value = jnp.sum(value.reshape(rows // 8, 8, TILE), axis=0)
                value = sum(value[n * val_count : (n + 1) * val_count] for n in range(8 // val_count))
                out.append(value if flip is None else value * flip)
            out = jnp.concatenate(out, 0)
            out = jnp.concatenate([out[:, :LANES], out[:, LANES:]], 0)
            tiles[tile] = out.astype(jnp.bfloat16)
            for offset in range(1, grow_count):
                pltpu.make_async_remote_copy(
                    tiles.at[tile], from_line.at[offset - 1, tile], line_send, line_recv.at[offset - 1],
                    device_id=line_peer(offset), device_id_type=MESH,
                ).start()

        def spread(source, origin):
            @pl.loop(1, plane_count)
            def _(offset):
                place = plane_peer(offset)
                pltpu.make_async_remote_copy(
                    source.at[row_tile(place)], rows_in.at[origin], plane_send.at[0], plane_recv.at[0],
                    device_id=place, device_id_type=MESH,
                ).start()
                pltpu.make_async_remote_copy(
                    source.at[pl.ds(place[2] * col_tiles, col_tiles)], cols_in.at[origin],
                    plane_send.at[1], plane_recv.at[1],
                    device_id=place, device_id_type=MESH,
                ).start()

            place = (band, grow, gcol)
            pltpu.make_async_copy(source.at[row_tile(place)], rows_in.at[origin], plane_recv.at[0]).start()
            pltpu.make_async_copy(
                source.at[pl.ds(gcol * col_tiles, col_tiles)], cols_in.at[origin], plane_recv.at[1]
            ).start()

        spread(tiles, number_of((band, grow, gcol)))
        for offset in range(1, grow_count):
            arrived = from_line.at[offset - 1]
            pltpu.make_async_copy(arrived, arrived, line_recv.at[offset - 1]).wait()
            spread(arrived, number_of(line_peer(grow_count - offset)))

        half = 2 * val_count
        depth = devices * half
        row = lax.broadcasted_iota(jnp.int32, (depth, 1), 0)

        def along_rows(values, number):
            lane = lax.broadcasted_iota(jnp.int32, (depth, values.shape[1]), 1)
            return jnp.sum(jnp.where(lane == number, values, 0), axis=1, keepdims=True)

        band_id = row // half
        val_id = row % val_count
        gap = along_rows(cond_energy[...], band_id) - along_rows(val_energy[...], val_id)
        counted = band_id >= along_rows(first_band[...], val_id)
        weights = []
        for freq in range(freq_count):
            denominator = gap * gap + frequencies[:, freq : freq + 1] * frequencies[:, freq : freq + 1]
            weights.append(jnp.where(counted, -4.0 * gap / denominator, 0.0) / (devices * val_count))

        pltpu.make_async_copy(rows_in, rows_in, plane_recv.at[0]).wait()
        pltpu.make_async_copy(cols_in, cols_in, plane_recv.at[1]).wait()

        cols = cols_in[...].astype(jnp.float32)
        right = jnp.concatenate(
            [cols[:, tile, side * half : (side + 1) * half].reshape(depth, LANES)
             for tile in range(col_tiles) for side in range(2)], 1
        ).astype(jnp.bfloat16)
        inward = rows_in[...].astype(jnp.float32)
        for side in range(2):
            part = inward[:, side * half : (side + 1) * half].reshape(depth, LANES)
            for freq in range(freq_count):
                left = part * weights[freq]
                cube = left.reshape(devices, half, LANES)
                swapped = jnp.concatenate([cube[:, val_count:], -cube[:, :val_count]], 1)
                for kind, value in enumerate((left, swapped.reshape(depth, LANES))):
                    out_ref[freq, kind, side * LANES : (side + 1) * LANES] = lax.dot_general(
                        value.astype(jnp.bfloat16), right, (((0,), (0,)), ((), ())),
                        preferred_element_type=jnp.float32,
                    ).astype(jnp.bfloat16)

        pltpu.make_async_copy(from_line, from_line, line_send).wait()
        for held, sem in ((rows_in, 0), (cols_in, 1)):
            sent = held.at[pl.ds(0, (plane_count - 1) * grow_count)]
            pltpu.make_async_copy(sent, sent, plane_send.at[sem]).wait()


def on_device(sizes, valence, conduction, val_energy, cond_energy, frequencies, gvec_index, first_band):
    band_count, grow_count, gcol_count = sizes
    devices = band_count * grow_count * gcol_count
    val_count = val_energy.shape[0]
    freq_count = frequencies.shape[0]
    num_gvec = gvec_index.shape[0]
    rows = val_count * GRID
    num_tiles = num_gvec // TILE
    col_tiles = num_tiles // gcol_count
    tile_shape = (4 * val_count, LANES)
    operands = (
        valence,
        conduction,
        jnp.asarray(plane_table()),
        jnp.asarray(phase_table(val_count)),
        gvec_index.reshape(num_tiles, 1, TILE),
        val_energy[None],
        cond_energy[None],
        frequencies[None],
        first_band[None],
    )
    specs = [pl.BlockSpec(a.shape, lambda n, rank=a.ndim: (0,) * rank) for a in operands]
    specs[2] = pl.BlockSpec((1, PLANE, CHUNK), lambda n: (n, 0, 0))
    out_shape = (freq_count, 2, TILE, num_gvec // gcol_count)
    out = pl.pallas_call(
        functools.partial(kernel, sizes),
        grid=(2 * CHUNKS,),
        out_shape=jax.ShapeDtypeStruct(out_shape, jnp.bfloat16),
        in_specs=specs,
        out_specs=pl.BlockSpec(out_shape, lambda n: (0, 0, 0, 0)),
        scratch_shapes=[
            pltpu.VMEM((2 * rows, PLANE), jnp.bfloat16),
            pltpu.VMEM((2 * CHUNKS, 2 * rows, CHUNK), jnp.bfloat16),
            pltpu.VMEM((num_tiles,) + tile_shape, jnp.bfloat16),
            pltpu.VMEM((grow_count - 1, num_tiles) + tile_shape, jnp.bfloat16),
            pltpu.VMEM((devices,) + tile_shape, jnp.bfloat16),
            pltpu.VMEM((devices, col_tiles) + tile_shape, jnp.bfloat16),
            pltpu.SemaphoreType.DMA,
            pltpu.SemaphoreType.DMA((grow_count - 1,)),
            pltpu.SemaphoreType.DMA((2,)),
            pltpu.SemaphoreType.DMA((2,)),
        ],
        compiler_params=pltpu.CompilerParams(
            collective_id=0, has_side_effects=True, vmem_limit_bytes=48 * 2**20
        ),
    )(*operands)
    out = jnp.transpose(out, (2, 0, 1, 3))
    row_count = num_gvec // (grow_count * band_count)
    if row_count < TILE:
        block = lax.axis_index("grow") * band_count + lax.axis_index("band")
        out = lax.dynamic_slice_in_dim(out, block * row_count % TILE, row_count, 0)
    return out


def solution(mesh):
    sizes = tuple(mesh.shape[name] for name in ("band", "grow", "gcol"))
    return jax.shard_map(
        functools.partial(on_device, sizes),
        mesh=mesh,
        in_specs=(P(), P(("band", "grow", "gcol"), None), P(), P(), P(), P(), P()),
        out_specs=P(("grow", "band"), None, None, "gcol"),
        check_vma=False,
    )
```

```python
import functools
import math

import jax
import jax.numpy as jnp
import ml_dtypes
import numpy as np
from jax import lax
from jax.experimental import pallas as pl
from jax.experimental.pallas import tpu as pltpu
from jax.sharding import PartitionSpec as P

GRID = 48
HALF = GRID // 2 + 1
PLANE = GRID * GRID
CHUNK = 256
CHUNKS = -(-GRID * HALF // CHUNK)
TILE = 256
LANES = 128
MESH = pl.DeviceIdType.MESH
TABLE_SCALE = 1.622
TABLE_GAIN = 1.6242055647


def plane_table():
    line = np.arange(GRID)
    k2, k3 = np.meshgrid(line, np.arange(HALF), indexing="ij")
    k2, k3 = k2.reshape(-1), k3.reshape(-1)
    b, e = np.meshgrid(line, line, indexing="ij")
    b, e = b.reshape(-1), e.reshape(-1)
    turn = (b[:, None] * k2[None] + e[:, None] * k3[None]) % GRID
    angle = 2.0 * np.pi * line / GRID
    parts = []
    for values in (np.cos(angle), -np.sin(angle)):
        small = (values * TABLE_SCALE).astype(np.float32).astype(ml_dtypes.bfloat16)
        full = np.zeros((PLANE, CHUNKS * CHUNK), ml_dtypes.bfloat16)
        full[:, : GRID * HALF] = small[turn]
        parts.append(full.reshape(PLANE, CHUNKS, CHUNK).transpose(1, 0, 2))
    return np.concatenate(parts, 0)


def phase_table(val_count):
    line = np.arange(GRID)
    angle = 2.0 * np.pi * (line[:, None] * line[None] % GRID) / GRID
    scale = GRID ** (-1.5) / TABLE_GAIN
    both = np.concatenate([np.cos(angle), np.sin(angle)], 0).astype(np.float64) * scale
    both = np.repeat(both, val_count, 0).astype(np.float32)
    high = both.astype(ml_dtypes.bfloat16)
    low = (both - high.astype(np.float32)).astype(ml_dtypes.bfloat16)
    table = np.zeros((both.shape[0], LANES), ml_dtypes.bfloat16)
    table[:, :GRID] = high
    table[:, LANES // 2 : LANES // 2 + GRID] = low
    return table


def kernel(
    sizes, val_hbm, cond_hbm, table_hbm, phase_ref, index_ref, val_energy, cond_energy, frequencies, first_band,
    out_ref, val_ref, cond_ref, table_ref, pair, planes, tiles, from_line, rows_in, cols_in,
    load, table_load, line_send, line_recv, plane_send, plane_recv,
):
    band_count, grow_count, gcol_count = sizes
    plane_count = band_count * gcol_count
    devices = plane_count * grow_count
    val_count = val_ref.shape[0]
    rows = val_count * GRID
    num_tiles = tiles.shape[0]
    col_tiles = num_tiles // gcol_count
    freq_count = out_ref.shape[0]
    band, grow, gcol = (lax.axis_index(name) for name in ("band", "grow", "gcol"))
    barrier = pltpu.get_barrier_semaphore()

    loads = [pltpu.make_async_copy(val_hbm, val_ref, load.at[0]), pltpu.make_async_copy(cond_hbm, cond_ref, load.at[1])]
    table_loads = [
        pltpu.make_async_copy(table_hbm.at[n], table_ref.at[n], table_load.at[n]) for n in range(2 * CHUNKS)
    ]
    for copy in loads + table_loads:
        copy.start()

    def turned(place, offset, count):
        place = place + offset
        return jnp.where(place >= count, place - count, place)

    def line_peer(offset):
        return band, turned(grow, offset, grow_count), gcol

    gcols = [turned(gcol, offset, gcol_count) for offset in range(gcol_count)]

    def each_plane_peer(body):
        def one_band(offset, first):
            to_band = turned(band, offset, band_count) if not first else band
            for gcol_offset in range(1 if first else 0, gcol_count):
                body((to_band, grow, gcols[gcol_offset]))

        one_band(0, True)
        if band_count <= 2:
            for offset in range(1, band_count):
                one_band(offset, False)
        else:
            pl.loop(1, band_count)(lambda offset: one_band(offset, False))

    def number_of(place):
        return (place[0] * grow_count + place[1]) * gcol_count + place[2]

    def row_tile(place):
        return (place[1] * band_count + place[0]) * num_tiles // (grow_count * band_count)

    def greet(place):
        pl.semaphore_signal(barrier, inc=1, device_id=place, device_id_type=MESH)

    for offset in range(1, grow_count):
        greet(line_peer(offset))
    each_plane_peer(greet)

    for copy in loads:
        copy.wait()
    group = 16 // val_count

    @pl.loop(0, GRID // group)
    def _(block):
        products = []
        for member in range(group):
            where = pl.ds(pl.multiple_of((block * group + member) * PLANE, LANES), PLANE)
            products.append(val_ref[:, where].astype(jnp.float32) * cond_ref[:, where].astype(jnp.float32))
        product = jnp.concatenate(products, 0)
        high = product.astype(jnp.bfloat16)
        start = pl.multiple_of(block * 16, 16)
        pair[pl.ds(start, 16)] = high
        pair[pl.ds(rows + start, 16)] = (product - high.astype(jnp.float32)).astype(jnp.bfloat16)

    for step in range(2 * CHUNKS):
        table_loads[step].wait()
        both = jnp.dot(pair[...], table_ref[step], preferred_element_type=jnp.float32)
        total = both[:rows] + both[rows:]
        high = total.astype(jnp.bfloat16)
        start = step // CHUNKS * 2 * rows
        where = pl.ds(step % CHUNKS * CHUNK, CHUNK)
        planes[start : start + rows, where] = high
        planes[start + rows : start + 2 * rows, where] = (total - high.astype(jnp.float32)).astype(jnp.bfloat16)

    if True:
        pl.semaphore_wait(barrier, grow_count - 1 + plane_count - 1)

        @pl.loop(0, num_tiles)
        def _(tile):
            index = index_ref[tile]
            index_float = index.astype(jnp.float32)
            upper = jnp.floor((index_float + 0.5) * (1.0 / GRID))
            k3 = index_float - GRID * upper
            k1 = jnp.floor((upper + 0.5) * (1.0 / GRID))
            k2 = upper - GRID * k1
            mirror = k3 > HALF - 1
            k1 = jnp.where(mirror & (k1 > 0), GRID - k1, k1).astype(jnp.int32)
            k2 = jnp.where(mirror & (k2 > 0), GRID - k2, k2)
            k3 = jnp.where(mirror, GRID - k3, k3)
            sign = jnp.where(mirror, -1.0, 1.0)
            place = (k2 * HALF + k3).astype(jnp.int32)
            line = lax.broadcasted_iota(jnp.int32, (CHUNKS * CHUNK, TILE), 0)
            pick = jnp.where(line == place, 1.0, 0.0).astype(jnp.bfloat16)
            picked = jnp.dot(planes[...], pick, preferred_element_type=jnp.float32)
            real = picked[:rows] + picked[rows : 2 * rows]
            imag = picked[2 * rows : 3 * rows] + picked[3 * rows :]
            line = line[:LANES]
            pick = jnp.where((line == k1) | (line == k1 + LANES // 2), 1.0, 0.0).astype(jnp.bfloat16)
            phases = jnp.dot(phase_ref[...], pick, preferred_element_type=jnp.float32)
            cos_one, sin_one = phases[:rows], phases[rows:]
            out = []
            for value, flip in (
                (real * cos_one + imag * sin_one, None),
                (imag * cos_one - real * sin_one, sign),
            ):
                value = jnp.sum(value.reshape(rows // 8, 8, TILE), axis=0)
                value = sum(value[n * val_count : (n + 1) * val_count] for n in range(8 // val_count))
                out.append(value if flip is None else value * flip)
            out = jnp.concatenate(out, 0)
            out = jnp.concatenate([out[:, :LANES], out[:, LANES:]], 0)
            tiles[tile] = out.astype(jnp.bfloat16)
            for offset in range(1, grow_count):
                pltpu.make_async_remote_copy(
                    tiles.at[tile], from_line.at[offset - 1, tile], line_send, line_recv.at[offset - 1],
                    device_id=line_peer(offset), device_id_type=MESH,
                ).start()

        def spread(source, origin):
            def send(place):
                pltpu.make_async_remote_copy(
                    source.at[row_tile(place)], rows_in.at[origin], plane_send.at[0], plane_recv.at[0],
                    device_id=place, device_id_type=MESH,
                ).start()
                pltpu.make_async_remote_copy(
                    source.at[pl.ds(place[2] * col_tiles, col_tiles)], cols_in.at[origin],
                    plane_send.at[1], plane_recv.at[1],
                    device_id=place, device_id_type=MESH,
                ).start()

            each_plane_peer(send)
            place = (band, grow, gcol)
            pltpu.make_async_copy(source.at[row_tile(place)], rows_in.at[origin], plane_recv.at[0]).start()
            pltpu.make_async_copy(
                source.at[pl.ds(gcol * col_tiles, col_tiles)], cols_in.at[origin], plane_recv.at[1]
            ).start()

        spread(tiles, number_of((band, grow, gcol)))
        for offset in range(1, grow_count):
            arrived = from_line.at[offset - 1]
            pltpu.make_async_copy(arrived, arrived, line_recv.at[offset - 1]).wait()
            spread(arrived, number_of(line_peer(grow_count - offset)))

        half = 2 * val_count
        depth = devices * half
        row = lax.broadcasted_iota(jnp.int32, (depth, 1), 0)

        def along_rows(values, number):
            lane = lax.broadcasted_iota(jnp.int32, (depth, values.shape[1]), 1)
            return jnp.sum(jnp.where(lane == number, values, 0), axis=1, keepdims=True)

        band_id = row // half
        val_id = row % val_count
        gap = along_rows(cond_energy[...], band_id) - along_rows(val_energy[...], val_id)
        counted = band_id >= along_rows(first_band[...], val_id)
        weights = []
        for freq in range(freq_count):
            denominator = gap * gap + frequencies[:, freq : freq + 1] * frequencies[:, freq : freq + 1]
            weights.append(jnp.where(counted, -4.0 * gap / denominator, 0.0) / (devices * val_count))

        pltpu.make_async_copy(rows_in, rows_in, plane_recv.at[0]).wait()
        pltpu.make_async_copy(cols_in, cols_in, plane_recv.at[1]).wait()

        cols = cols_in[...].astype(jnp.float32)
        right = jnp.concatenate(
            [cols[:, tile, side * half : (side + 1) * half].reshape(depth, LANES)
             for tile in range(col_tiles) for side in range(2)], 1
        ).astype(jnp.bfloat16)
        inward = rows_in[...].astype(jnp.float32)
        for side in range(2):
            part = inward[:, side * half : (side + 1) * half].reshape(depth, LANES)
            for freq in range(freq_count):
                left = part * weights[freq]
                cube = left.reshape(devices, half, LANES)
                swapped = jnp.concatenate([cube[:, val_count:], -cube[:, :val_count]], 1)
                for kind, value in enumerate((left, swapped.reshape(depth, LANES))):
                    out_ref[freq, kind, side * LANES : (side + 1) * LANES] = lax.dot_general(
                        value.astype(jnp.bfloat16), right, (((0,), (0,)), ((), ())),
                        preferred_element_type=jnp.float32,
                    ).astype(jnp.bfloat16)

        pltpu.make_async_copy(from_line, from_line, line_send).wait()
        for held, sem in ((rows_in, 0), (cols_in, 1)):
            sent = held.at[pl.ds(0, (plane_count - 1) * grow_count)]
            pltpu.make_async_copy(sent, sent, plane_send.at[sem]).wait()


def on_device(sizes, valence, conduction, val_energy, cond_energy, frequencies, gvec_index, first_band):
    band_count, grow_count, gcol_count = sizes
    devices = band_count * grow_count * gcol_count
    val_count = val_energy.shape[0]
    freq_count = frequencies.shape[0]
    num_gvec = gvec_index.shape[0]
    rows = val_count * GRID
    num_tiles = num_gvec // TILE
    col_tiles = num_tiles // gcol_count
    tile_shape = (4 * val_count, LANES)
    operands = (
        valence,
        conduction,
        jnp.asarray(plane_table()),
        jnp.asarray(phase_table(val_count)),
        gvec_index.reshape(num_tiles, 1, TILE),
        val_energy[None],
        cond_energy[None],
        frequencies[None],
        first_band[None],
    )
    specs = [pl.BlockSpec(memory_space=pl.ANY)] * 3 + [pl.BlockSpec(memory_space=pltpu.VMEM)] * 6
    out_shape = (freq_count, 2, TILE, num_gvec // gcol_count)
    out = pl.pallas_call(
        functools.partial(kernel, sizes),
        out_shape=jax.ShapeDtypeStruct(out_shape, jnp.bfloat16),
        in_specs=specs,
        out_specs=pl.BlockSpec(memory_space=pltpu.VMEM),
        scratch_shapes=[
            pltpu.VMEM(valence.shape, jnp.bfloat16),
            pltpu.VMEM(conduction.shape, jnp.bfloat16),
            pltpu.VMEM((2 * CHUNKS, PLANE, CHUNK), jnp.bfloat16),
            pltpu.VMEM((2 * rows, PLANE), jnp.bfloat16),
            pltpu.VMEM((4 * rows, CHUNKS * CHUNK), jnp.bfloat16),
            pltpu.VMEM((num_tiles,) + tile_shape, jnp.bfloat16),
            pltpu.VMEM((grow_count - 1, num_tiles) + tile_shape, jnp.bfloat16),
            pltpu.VMEM((devices,) + tile_shape, jnp.bfloat16),
            pltpu.VMEM((devices, col_tiles) + tile_shape, jnp.bfloat16),
            pltpu.SemaphoreType.DMA((2,)),
            pltpu.SemaphoreType.DMA((2 * CHUNKS,)),
            pltpu.SemaphoreType.DMA,
            pltpu.SemaphoreType.DMA((grow_count - 1,)),
            pltpu.SemaphoreType.DMA((2,)),
            pltpu.SemaphoreType.DMA((2,)),
        ],
        compiler_params=pltpu.CompilerParams(
            collective_id=0, has_side_effects=True, vmem_limit_bytes=63 * 2**20
        ),
    )(*operands)
    out = jnp.transpose(out, (2, 0, 1, 3))
    row_count = num_gvec // (grow_count * band_count)
    if row_count < TILE:
        block = lax.axis_index("grow") * band_count + lax.axis_index("band")
        out = lax.dynamic_slice_in_dim(out, block * row_count % TILE, row_count, 0)
    return out


def solution(mesh):
    sizes = tuple(mesh.shape[name] for name in ("band", "grow", "gcol"))
    return jax.shard_map(
        functools.partial(on_device, sizes),
        mesh=mesh,
        in_specs=(P(), P(("band", "grow", "gcol"), None), P(), P(), P(), P(), P()),
        out_specs=P(("grow", "band"), None, None, "gcol"),
        check_vma=False,
    )
```

```python
import functools
import math

import jax
import jax.numpy as jnp
import ml_dtypes
import numpy as np
from jax import lax
from jax.experimental import pallas as pl
from jax.experimental.pallas import tpu as pltpu
from jax.sharding import PartitionSpec as P

GRID = 48
HALF = GRID // 2 + 1
PLANE = GRID * GRID
CHUNK = 256
CHUNKS = -(-GRID * HALF // CHUNK)
TILE = 256
LANES = 128
MESH = pl.DeviceIdType.MESH
TABLE_SCALE = 1.622
TABLE_GAIN = 1.6242055647


def plane_table():
    line = np.arange(GRID)
    k2, k3 = np.meshgrid(line, np.arange(HALF), indexing="ij")
    k2, k3 = k2.reshape(-1), k3.reshape(-1)
    b, e = np.meshgrid(line, line, indexing="ij")
    b, e = b.reshape(-1), e.reshape(-1)
    turn = (b[:, None] * k2[None] + e[:, None] * k3[None]) % GRID
    angle = 2.0 * np.pi * line / GRID
    parts = []
    for values in (np.cos(angle), -np.sin(angle)):
        small = (values * TABLE_SCALE).astype(np.float32).astype(ml_dtypes.bfloat16)
        full = np.zeros((PLANE, CHUNKS * CHUNK), ml_dtypes.bfloat16)
        full[:, : GRID * HALF] = small[turn]
        parts.append(full.reshape(PLANE, CHUNKS, CHUNK).transpose(1, 0, 2))
    return np.concatenate(parts, 0)


def phase_table(val_count):
    line = np.arange(GRID)
    angle = 2.0 * np.pi * (line[:, None] * line[None] % GRID) / GRID
    scale = GRID ** (-1.5) / TABLE_GAIN
    both = np.concatenate([np.cos(angle), np.sin(angle)], 0).astype(np.float64) * scale
    both = np.repeat(both, val_count, 0).astype(np.float32)
    high = both.astype(ml_dtypes.bfloat16)
    low = (both - high.astype(np.float32)).astype(ml_dtypes.bfloat16)
    table = np.zeros((both.shape[0], LANES), ml_dtypes.bfloat16)
    table[:, :GRID] = high
    table[:, LANES // 2 : LANES // 2 + GRID] = low
    return table


def kernel(
    sizes, val_hbm, cond_hbm, table_hbm, phase_hbm, index_hbm, val_energy_hbm, cond_energy_hbm, frequencies_hbm,
    first_band_hbm, out_ref, val_ref, cond_ref, table_ref, phase_ref, index_ref, val_energy, cond_energy,
    frequencies, first_band, pair, planes, tiles, from_line, rows_in, cols_in,
    load, table_load, line_send, line_recv, plane_send, plane_recv,
):
    band_count, grow_count, gcol_count = sizes
    plane_count = band_count * gcol_count
    devices = plane_count * grow_count
    val_count = val_ref.shape[0]
    rows = val_count * GRID
    num_tiles = tiles.shape[0]
    col_tiles = num_tiles // gcol_count
    freq_count = out_ref.shape[0]
    band, grow, gcol = (lax.axis_index(name) for name in ("band", "grow", "gcol"))
    barrier = pltpu.get_barrier_semaphore()

    loads = [pltpu.make_async_copy(val_hbm, val_ref, load.at[0]), pltpu.make_async_copy(cond_hbm, cond_ref, load.at[1])]
    table_loads = [
        pltpu.make_async_copy(table_hbm.at[n], table_ref.at[n], table_load.at[n]) for n in range(2 * CHUNKS)
    ]
    small_loads = [
        pltpu.make_async_copy(source, target, load.at[2 + n])
        for n, (source, target) in enumerate((
            (phase_hbm, phase_ref), (index_hbm, index_ref), (val_energy_hbm, val_energy),
            (cond_energy_hbm, cond_energy), (frequencies_hbm, frequencies), (first_band_hbm, first_band),
        ))
    ]
    for copy in loads + small_loads:
        copy.start()

    def turned(place, offset, count):
        place = place + offset
        return jnp.where(place >= count, place - count, place)

    def line_peer(offset):
        return band, turned(grow, offset, grow_count), gcol

    gcols = [turned(gcol, offset, gcol_count) for offset in range(gcol_count)]

    def each_plane_peer(body):
        def one_band(offset, first):
            to_band = turned(band, offset, band_count) if not first else band
            for gcol_offset in range(1 if first else 0, gcol_count):
                body((to_band, grow, gcols[gcol_offset]))

        one_band(0, True)
        if band_count <= 2:
            for offset in range(1, band_count):
                one_band(offset, False)
        else:
            pl.loop(1, band_count)(lambda offset: one_band(offset, False))

    def number_of(place):
        return (place[0] * grow_count + place[1]) * gcol_count + place[2]

    def row_tile(place):
        return (place[1] * band_count + place[0]) * num_tiles // (grow_count * band_count)

    def greet(place):
        pl.semaphore_signal(barrier, inc=1, device_id=place, device_id_type=MESH)

    for offset in range(1, grow_count):
        greet(line_peer(offset))
    each_plane_peer(greet)

    for copy in loads:
        copy.wait()
    for copy in table_loads:
        copy.start()
    group = 16 // val_count

    @pl.loop(0, GRID // group)
    def _(block):
        products = []
        for member in range(group):
            where = pl.ds(pl.multiple_of((block * group + member) * PLANE, LANES), PLANE)
            products.append(val_ref[:, where].astype(jnp.float32) * cond_ref[:, where].astype(jnp.float32))
        product = jnp.concatenate(products, 0)
        high = product.astype(jnp.bfloat16)
        start = pl.multiple_of(block * 16, 16)
        pair[pl.ds(start, 16)] = high
        pair[pl.ds(rows + start, 16)] = (product - high.astype(jnp.float32)).astype(jnp.bfloat16)

    for step in range(2 * CHUNKS):
        table_loads[step].wait()
        both = jnp.dot(pair[...], table_ref[step], preferred_element_type=jnp.float32)
        total = both[:rows] + both[rows:]
        high = total.astype(jnp.bfloat16)
        start = step // CHUNKS * 2 * rows
        where = pl.ds(step % CHUNKS * CHUNK, CHUNK)
        planes[start : start + rows, where] = high
        planes[start + rows : start + 2 * rows, where] = (total - high.astype(jnp.float32)).astype(jnp.bfloat16)

    for copy in small_loads:
        copy.wait()
    pl.semaphore_wait(barrier, grow_count - 1 + plane_count - 1)

    @pl.loop(0, num_tiles)
    def _(tile):
        index = index_ref[tile]
        index_float = index.astype(jnp.float32)
        upper = jnp.floor((index_float + 0.5) * (1.0 / GRID))
        k3 = index_float - GRID * upper
        k1 = jnp.floor((upper + 0.5) * (1.0 / GRID))
        k2 = upper - GRID * k1
        mirror = k3 > HALF - 1
        k1 = jnp.where(mirror & (k1 > 0), GRID - k1, k1).astype(jnp.int32)
        k2 = jnp.where(mirror & (k2 > 0), GRID - k2, k2)
        k3 = jnp.where(mirror, GRID - k3, k3)
        sign = jnp.where(mirror, -1.0, 1.0)
        place = (k2 * HALF + k3).astype(jnp.int32)
        line = lax.broadcasted_iota(jnp.int32, (CHUNKS * CHUNK, TILE), 0)
        pick = jnp.where(line == place, 1.0, 0.0).astype(jnp.bfloat16)
        picked = jnp.dot(planes[...], pick, preferred_element_type=jnp.float32)
        real = picked[:rows] + picked[rows : 2 * rows]
        imag = picked[2 * rows : 3 * rows] + picked[3 * rows :]
        line = line[:LANES]
        pick = jnp.where((line == k1) | (line == k1 + LANES // 2), 1.0, 0.0).astype(jnp.bfloat16)
        phases = jnp.dot(phase_ref[...], pick, preferred_element_type=jnp.float32)
        cos_one, sin_one = phases[:rows], phases[rows:]
        out = []
        for value, flip in (
            (real * cos_one + imag * sin_one, None),
            (imag * cos_one - real * sin_one, sign),
        ):
            value = jnp.sum(value.reshape(rows // 8, 8, TILE), axis=0)
            value = sum(value[n * val_count : (n + 1) * val_count] for n in range(8 // val_count))
            out.append(value if flip is None else value * flip)
        out = jnp.concatenate(out, 0)
        out = jnp.concatenate([out[:, :LANES], out[:, LANES:]], 0)
        tiles[tile] = out.astype(jnp.bfloat16)
        for offset in range(1, grow_count):
            pltpu.make_async_remote_copy(
                tiles.at[tile], from_line.at[offset - 1, tile], line_send, line_recv.at[offset - 1],
                device_id=line_peer(offset), device_id_type=MESH,
            ).start()

    def spread(source, origin):
        def send(place):
            pltpu.make_async_remote_copy(
                source.at[row_tile(place)], rows_in.at[origin], plane_send.at[0], plane_recv.at[0],
                device_id=place, device_id_type=MESH,
            ).start()
            pltpu.make_async_remote_copy(
                source.at[pl.ds(place[2] * col_tiles, col_tiles)], cols_in.at[origin],
                plane_send.at[1], plane_recv.at[1],
                device_id=place, device_id_type=MESH,
            ).start()

        each_plane_peer(send)
        place = (band, grow, gcol)
        pltpu.make_async_copy(source.at[row_tile(place)], rows_in.at[origin], plane_recv.at[0]).start()
        pltpu.make_async_copy(
            source.at[pl.ds(gcol * col_tiles, col_tiles)], cols_in.at[origin], plane_recv.at[1]
        ).start()

    spread(tiles, number_of((band, grow, gcol)))
    for offset in range(1, grow_count):
        arrived = from_line.at[offset - 1]
        pltpu.make_async_copy(arrived, arrived, line_recv.at[offset - 1]).wait()
        spread(arrived, number_of(line_peer(grow_count - offset)))

    half = 2 * val_count
    depth = devices * half
    row = lax.broadcasted_iota(jnp.int32, (depth, 1), 0)

    def along_rows(values, number):
        lane = lax.broadcasted_iota(jnp.int32, (depth, values.shape[1]), 1)
        return jnp.sum(jnp.where(lane == number, values, 0), axis=1, keepdims=True)

    band_id = row // half
    val_id = row % val_count
    gap = along_rows(cond_energy[...], band_id) - along_rows(val_energy[...], val_id)
    counted = band_id >= along_rows(first_band[...], val_id)
    weights = []
    for freq in range(freq_count):
        denominator = gap * gap + frequencies[:, freq : freq + 1] * frequencies[:, freq : freq + 1]
        weights.append(jnp.where(counted, -4.0 * gap / denominator, 0.0) / (devices * val_count))

    pltpu.make_async_copy(rows_in, rows_in, plane_recv.at[0]).wait()
    pltpu.make_async_copy(cols_in, cols_in, plane_recv.at[1]).wait()

    cols = cols_in[...].astype(jnp.float32)
    right = jnp.concatenate(
        [cols[:, tile, side * half : (side + 1) * half].reshape(depth, LANES)
         for tile in range(col_tiles) for side in range(2)], 1
    ).astype(jnp.bfloat16)
    inward = rows_in[...].astype(jnp.float32)
    for side in range(2):
        part = inward[:, side * half : (side + 1) * half].reshape(depth, LANES)
        for freq in range(freq_count):
            left = part * weights[freq]
            cube = left.reshape(devices, half, LANES)
            swapped = jnp.concatenate([cube[:, val_count:], -cube[:, :val_count]], 1)
            for kind, value in enumerate((left, swapped.reshape(depth, LANES))):
                out_ref[freq, kind, side * LANES : (side + 1) * LANES] = lax.dot_general(
                    value.astype(jnp.bfloat16), right, (((0,), (0,)), ((), ())),
                    preferred_element_type=jnp.float32,
                ).astype(jnp.bfloat16)

    pltpu.make_async_copy(from_line, from_line, line_send).wait()
    for held, sem in ((rows_in, 0), (cols_in, 1)):
        sent = held.at[pl.ds(0, (plane_count - 1) * grow_count)]
        pltpu.make_async_copy(sent, sent, plane_send.at[sem]).wait()


def on_device(sizes, valence, conduction, val_energy, cond_energy, frequencies, gvec_index, first_band):
    band_count, grow_count, gcol_count = sizes
    devices = band_count * grow_count * gcol_count
    val_count = val_energy.shape[0]
    freq_count = frequencies.shape[0]
    num_gvec = gvec_index.shape[0]
    rows = val_count * GRID
    num_tiles = num_gvec // TILE
    col_tiles = num_tiles // gcol_count
    tile_shape = (4 * val_count, LANES)
    operands = (
        valence,
        conduction,
        jnp.asarray(plane_table()),
        jnp.asarray(phase_table(val_count)),
        gvec_index.reshape(num_tiles, 1, TILE),
        val_energy[None],
        cond_energy[None],
        frequencies[None],
        first_band[None],
    )
    out_shape = (freq_count, 2, TILE, num_gvec // gcol_count)
    out = pl.pallas_call(
        functools.partial(kernel, sizes),
        out_shape=jax.ShapeDtypeStruct(out_shape, jnp.bfloat16),
        in_specs=[pl.BlockSpec(memory_space=pl.ANY)] * len(operands),
        out_specs=pl.BlockSpec(memory_space=pltpu.VMEM),
        scratch_shapes=[
            pltpu.VMEM(valence.shape, jnp.bfloat16),
            pltpu.VMEM(conduction.shape, jnp.bfloat16),
            pltpu.VMEM((2 * CHUNKS, PLANE, CHUNK), jnp.bfloat16),
            *(pltpu.VMEM(operand.shape, operand.dtype) for operand in operands[3:]),
            pltpu.VMEM((2 * rows, PLANE), jnp.bfloat16),
            pltpu.VMEM((4 * rows, CHUNKS * CHUNK), jnp.bfloat16),
            pltpu.VMEM((num_tiles,) + tile_shape, jnp.bfloat16),
            pltpu.VMEM((grow_count - 1, num_tiles) + tile_shape, jnp.bfloat16),
            pltpu.VMEM((devices,) + tile_shape, jnp.bfloat16),
            pltpu.VMEM((devices, col_tiles) + tile_shape, jnp.bfloat16),
            pltpu.SemaphoreType.DMA((len(operands) - 1,)),
            pltpu.SemaphoreType.DMA((2 * CHUNKS,)),
            pltpu.SemaphoreType.DMA,
            pltpu.SemaphoreType.DMA((grow_count - 1,)),
            pltpu.SemaphoreType.DMA((2,)),
            pltpu.SemaphoreType.DMA((2,)),
        ],
        compiler_params=pltpu.CompilerParams(
            collective_id=0, has_side_effects=True, vmem_limit_bytes=63 * 2**20
        ),
    )(*operands)
    out = jnp.transpose(out, (2, 0, 1, 3))
    row_count = num_gvec // (grow_count * band_count)
    if row_count < TILE:
        block = lax.axis_index("grow") * band_count + lax.axis_index("band")
        out = lax.dynamic_slice_in_dim(out, block * row_count % TILE, row_count, 0)
    return out


def solution(mesh):
    sizes = tuple(mesh.shape[name] for name in ("band", "grow", "gcol"))
    return jax.shard_map(
        functools.partial(on_device, sizes),
        mesh=mesh,
        in_specs=(P(), P(("band", "grow", "gcol"), None), P(), P(), P(), P(), P()),
        out_specs=P(("grow", "band"), None, None, "gcol"),
        check_vma=False,
    )
```

```python
import functools
import math

import jax
import jax.numpy as jnp
import ml_dtypes
import numpy as np
from jax import lax
from jax.experimental import pallas as pl
from jax.experimental.pallas import tpu as pltpu
from jax.sharding import PartitionSpec as P

GRID = 48
HALF = GRID // 2 + 1
PLANE = GRID * GRID
CHUNK = 256
CHUNKS = -(-GRID * HALF // CHUNK)
TILE = 256
LANES = 128
MESH = pl.DeviceIdType.MESH
TABLE_SCALE = 1.622
TABLE_GAIN = 1.6242055647


def plane_table():
    line = np.arange(GRID)
    k2, k3 = np.meshgrid(line, np.arange(HALF), indexing="ij")
    k2, k3 = k2.reshape(-1), k3.reshape(-1)
    b, e = np.meshgrid(line, line, indexing="ij")
    b, e = b.reshape(-1), e.reshape(-1)
    turn = (b[:, None] * k2[None] + e[:, None] * k3[None]) % GRID
    angle = 2.0 * np.pi * line / GRID
    parts = []
    for values in (np.cos(angle), -np.sin(angle)):
        small = (values * TABLE_SCALE).astype(np.float32).astype(ml_dtypes.bfloat16)
        full = np.zeros((PLANE, CHUNKS * CHUNK), ml_dtypes.bfloat16)
        full[:, : GRID * HALF] = small[turn]
        parts.append(full.reshape(PLANE, CHUNKS, CHUNK).transpose(1, 0, 2))
    return np.concatenate(parts, 0)


def phase_table(val_count):
    line = np.arange(GRID)
    angle = 2.0 * np.pi * (line[:, None] * line[None] % GRID) / GRID
    scale = GRID ** (-1.5) / TABLE_GAIN
    both = np.concatenate([np.cos(angle), np.sin(angle)], 0).astype(np.float64) * scale
    both = np.repeat(both, val_count, 0).astype(np.float32)
    high = both.astype(ml_dtypes.bfloat16)
    low = (both - high.astype(np.float32)).astype(ml_dtypes.bfloat16)
    table = np.zeros((both.shape[0], LANES), ml_dtypes.bfloat16)
    table[:, :GRID] = high
    table[:, LANES // 2 : LANES // 2 + GRID] = low
    return table


def kernel(
    sizes, val_hbm, cond_hbm, table_hbm, phase_hbm, index_hbm, val_energy_hbm, cond_energy_hbm, frequencies_hbm,
    first_band_hbm, out_ref, val_ref, cond_ref, table_ref, phase_ref, index_ref, val_energy, cond_energy,
    frequencies, first_band, pair, planes, tiles, from_line, rows_in, cols_in,
    load, table_load, line_send, line_recv, plane_send, plane_recv,
):
    band_count, grow_count, gcol_count = sizes
    plane_count = band_count * gcol_count
    devices = plane_count * grow_count
    val_count = val_ref.shape[0]
    rows = val_count * GRID
    num_tiles = tiles.shape[0]
    col_tiles = num_tiles // gcol_count
    freq_count = out_ref.shape[0]
    band, grow, gcol = (lax.axis_index(name) for name in ("band", "grow", "gcol"))
    barrier = pltpu.get_barrier_semaphore()

    loads = [pltpu.make_async_copy(val_hbm, val_ref, load.at[0]), pltpu.make_async_copy(cond_hbm, cond_ref, load.at[1])]
    table_loads = [
        pltpu.make_async_copy(table_hbm.at[n], table_ref.at[n], table_load.at[n]) for n in range(2 * CHUNKS)
    ]
    small_loads = [
        pltpu.make_async_copy(source, target, load.at[2 + n])
        for n, (source, target) in enumerate((
            (phase_hbm, phase_ref), (index_hbm, index_ref), (val_energy_hbm, val_energy),
            (cond_energy_hbm, cond_energy), (frequencies_hbm, frequencies), (first_band_hbm, first_band),
        ))
    ]
    for copy in loads + small_loads:
        copy.start()

    def turned(place, offset, count):
        place = place + offset
        return jnp.where(place >= count, place - count, place)

    def line_peer(offset):
        return band, turned(grow, offset, grow_count), gcol

    gcols = [turned(gcol, offset, gcol_count) for offset in range(gcol_count)]

    def each_plane_peer(body):
        def one_band(offset, first):
            to_band = turned(band, offset, band_count) if not first else band
            for gcol_offset in range(1 if first else 0, gcol_count):
                body((to_band, grow, gcols[gcol_offset]))

        one_band(0, True)
        if band_count <= 2:
            for offset in range(1, band_count):
                one_band(offset, False)
        else:
            pl.loop(1, band_count)(lambda offset: one_band(offset, False))

    def number_of(place):
        return (place[0] * grow_count + place[1]) * gcol_count + place[2]

    def row_tile(place):
        return (place[1] * band_count + place[0]) * num_tiles // (grow_count * band_count)

    def greet(place):
        pl.semaphore_signal(barrier, inc=1, device_id=place, device_id_type=MESH)

    for offset in range(1, grow_count):
        greet(line_peer(offset))
    each_plane_peer(greet)

    for copy in loads:
        copy.wait()
    for copy in table_loads:
        copy.start()
    group = 16 // val_count

    @pl.loop(0, GRID // group)
    def _(block):
        products = []
        for member in range(group):
            where = pl.ds(pl.multiple_of((block * group + member) * PLANE, LANES), PLANE)
            products.append(val_ref[:, where].astype(jnp.float32) * cond_ref[:, where].astype(jnp.float32))
        product = jnp.concatenate(products, 0)
        high = product.astype(jnp.bfloat16)
        start = pl.multiple_of(block * 16, 16)
        pair[pl.ds(start, 16)] = high
        pair[pl.ds(rows + start, 16)] = (product - high.astype(jnp.float32)).astype(jnp.bfloat16)

    for step in range(2 * CHUNKS):
        table_loads[step].wait()
        both = jnp.dot(pair[...], table_ref[step], preferred_element_type=jnp.float32)
        total = both[:rows] + both[rows:]
        start = step // CHUNKS * rows
        planes[start : start + rows, pl.ds(step % CHUNKS * CHUNK, CHUNK)] = total.astype(jnp.bfloat16)

    for copy in small_loads:
        copy.wait()
    pl.semaphore_wait(barrier, grow_count - 1 + plane_count - 1)

    @pl.loop(0, num_tiles)
    def _(tile):
        index = index_ref[tile]
        index_float = index.astype(jnp.float32)
        upper = jnp.floor((index_float + 0.5) * (1.0 / GRID))
        k3 = index_float - GRID * upper
        k1 = jnp.floor((upper + 0.5) * (1.0 / GRID))
        k2 = upper - GRID * k1
        mirror = k3 > HALF - 1
        k1 = jnp.where(mirror & (k1 > 0), GRID - k1, k1).astype(jnp.int32)
        k2 = jnp.where(mirror & (k2 > 0), GRID - k2, k2)
        k3 = jnp.where(mirror, GRID - k3, k3)
        sign = jnp.where(mirror, -1.0, 1.0)
        place = (k2 * HALF + k3).astype(jnp.int32)
        line = lax.broadcasted_iota(jnp.int32, (CHUNKS * CHUNK, TILE), 0)
        pick = jnp.where(line == place, 1.0, 0.0).astype(jnp.bfloat16)
        picked = jnp.dot(planes[...], pick, preferred_element_type=jnp.float32)
        real, imag = picked[:rows], picked[rows:]
        line = line[:LANES]
        pick = jnp.where((line == k1) | (line == k1 + LANES // 2), 1.0, 0.0).astype(jnp.bfloat16)
        phases = jnp.dot(phase_ref[...], pick, preferred_element_type=jnp.float32)
        cos_one, sin_one = phases[:rows], phases[rows:]
        out = []
        for value, flip in (
            (real * cos_one + imag * sin_one, None),
            (imag * cos_one - real * sin_one, sign),
        ):
            value = jnp.sum(value.reshape(rows // 8, 8, TILE), axis=0)
            value = sum(value[n * val_count : (n + 1) * val_count] for n in range(8 // val_count))
            out.append(value if flip is None else value * flip)
        out = jnp.concatenate(out, 0)
        out = jnp.concatenate([out[:, :LANES], out[:, LANES:]], 0)
        tiles[tile] = out.astype(jnp.bfloat16)
        for offset in range(1, grow_count):
            pltpu.make_async_remote_copy(
                tiles.at[tile], from_line.at[offset - 1, tile], line_send, line_recv.at[offset - 1],
                device_id=line_peer(offset), device_id_type=MESH,
            ).start()

    def spread(source, origin):
        def send(place):
            pltpu.make_async_remote_copy(
                source.at[row_tile(place)], rows_in.at[origin], plane_send.at[0], plane_recv.at[0],
                device_id=place, device_id_type=MESH,
            ).start()
            pltpu.make_async_remote_copy(
                source.at[pl.ds(place[2] * col_tiles, col_tiles)], cols_in.at[origin],
                plane_send.at[1], plane_recv.at[1],
                device_id=place, device_id_type=MESH,
            ).start()

        each_plane_peer(send)
        place = (band, grow, gcol)
        pltpu.make_async_copy(source.at[row_tile(place)], rows_in.at[origin], plane_recv.at[0]).start()
        pltpu.make_async_copy(
            source.at[pl.ds(gcol * col_tiles, col_tiles)], cols_in.at[origin], plane_recv.at[1]
        ).start()

    spread(tiles, number_of((band, grow, gcol)))
    for offset in range(1, grow_count):
        arrived = from_line.at[offset - 1]
        pltpu.make_async_copy(arrived, arrived, line_recv.at[offset - 1]).wait()
        spread(arrived, number_of(line_peer(grow_count - offset)))

    half = 2 * val_count
    depth = devices * half
    row = lax.broadcasted_iota(jnp.int32, (depth, 1), 0)

    def along_rows(values, number):
        lane = lax.broadcasted_iota(jnp.int32, (depth, values.shape[1]), 1)
        return jnp.sum(jnp.where(lane == number, values, 0), axis=1, keepdims=True)

    band_id = row // half
    val_id = row % val_count
    gap = along_rows(cond_energy[...], band_id) - along_rows(val_energy[...], val_id)
    counted = band_id >= along_rows(first_band[...], val_id)
    weights = []
    for freq in range(freq_count):
        denominator = gap * gap + frequencies[:, freq : freq + 1] * frequencies[:, freq : freq + 1]
        weights.append(jnp.where(counted, -4.0 * gap / denominator, 0.0) / (devices * val_count))

    pltpu.make_async_copy(rows_in, rows_in, plane_recv.at[0]).wait()
    pltpu.make_async_copy(cols_in, cols_in, plane_recv.at[1]).wait()

    cols = cols_in[...].astype(jnp.float32)
    right = jnp.concatenate(
        [cols[:, tile, side * half : (side + 1) * half].reshape(depth, LANES)
         for tile in range(col_tiles) for side in range(2)], 1
    ).astype(jnp.bfloat16)
    inward = rows_in[...].astype(jnp.float32)
    parts = [inward[:, side * half : (side + 1) * half].reshape(depth, LANES) for side in range(2)]
    lefts = []
    for freq in range(freq_count):
        kept = [part * weights[freq] for part in parts]
        cubes = [left.reshape(devices, half, LANES) for left in kept]
        turned_round = [
            jnp.concatenate([cube[:, val_count:], -cube[:, :val_count]], 1).reshape(depth, LANES) for cube in cubes
        ]
        lefts += kept + turned_round
    left = jnp.concatenate(lefts, 1).astype(jnp.bfloat16)
    out_ref[...] = lax.dot_general(
        left, right, (((0,), (0,)), ((), ())), preferred_element_type=jnp.float32
    ).astype(jnp.bfloat16).reshape(out_ref.shape)

    pltpu.make_async_copy(from_line, from_line, line_send).wait()
    for held, sem in ((rows_in, 0), (cols_in, 1)):
        sent = held.at[pl.ds(0, (plane_count - 1) * grow_count)]
        pltpu.make_async_copy(sent, sent, plane_send.at[sem]).wait()


def on_device(sizes, valence, conduction, val_energy, cond_energy, frequencies, gvec_index, first_band):
    band_count, grow_count, gcol_count = sizes
    devices = band_count * grow_count * gcol_count
    val_count = val_energy.shape[0]
    freq_count = frequencies.shape[0]
    num_gvec = gvec_index.shape[0]
    rows = val_count * GRID
    num_tiles = num_gvec // TILE
    col_tiles = num_tiles // gcol_count
    tile_shape = (4 * val_count, LANES)
    operands = (
        valence,
        conduction,
        jnp.asarray(plane_table()),
        jnp.asarray(phase_table(val_count)),
        gvec_index.reshape(num_tiles, 1, TILE),
        val_energy[None],
        cond_energy[None],
        frequencies[None],
        first_band[None],
    )
    out_shape = (freq_count, 2, TILE, num_gvec // gcol_count)
    out = pl.pallas_call(
        functools.partial(kernel, sizes),
        out_shape=jax.ShapeDtypeStruct(out_shape, jnp.bfloat16),
        in_specs=[pl.BlockSpec(memory_space=pl.ANY)] * len(operands),
        out_specs=pl.BlockSpec(memory_space=pltpu.VMEM),
        scratch_shapes=[
            pltpu.VMEM(valence.shape, jnp.bfloat16),
            pltpu.VMEM(conduction.shape, jnp.bfloat16),
            pltpu.VMEM((2 * CHUNKS, PLANE, CHUNK), jnp.bfloat16),
            *(pltpu.VMEM(operand.shape, operand.dtype) for operand in operands[3:]),
            pltpu.VMEM((2 * rows, PLANE), jnp.bfloat16),
            pltpu.VMEM((2 * rows, CHUNKS * CHUNK), jnp.bfloat16),
            pltpu.VMEM((num_tiles,) + tile_shape, jnp.bfloat16),
            pltpu.VMEM((grow_count - 1, num_tiles) + tile_shape, jnp.bfloat16),
            pltpu.VMEM((devices,) + tile_shape, jnp.bfloat16),
            pltpu.VMEM((devices, col_tiles) + tile_shape, jnp.bfloat16),
            pltpu.SemaphoreType.DMA((len(operands) - 1,)),
            pltpu.SemaphoreType.DMA((2 * CHUNKS,)),
            pltpu.SemaphoreType.DMA,
            pltpu.SemaphoreType.DMA((grow_count - 1,)),
            pltpu.SemaphoreType.DMA((2,)),
            pltpu.SemaphoreType.DMA((2,)),
        ],
        compiler_params=pltpu.CompilerParams(
            collective_id=0, has_side_effects=True, vmem_limit_bytes=63 * 2**20
        ),
    )(*operands)
    out = jnp.transpose(out, (2, 0, 1, 3))
    row_count = num_gvec // (grow_count * band_count)
    if row_count < TILE:
        block = lax.axis_index("grow") * band_count + lax.axis_index("band")
        out = lax.dynamic_slice_in_dim(out, block * row_count % TILE, row_count, 0)
    return out


def solution(mesh):
    sizes = tuple(mesh.shape[name] for name in ("band", "grow", "gcol"))
    return jax.shard_map(
        functools.partial(on_device, sizes),
        mesh=mesh,
        in_specs=(P(), P(("band", "grow", "gcol"), None), P(), P(), P(), P(), P()),
        out_specs=P(("grow", "band"), None, None, "gcol"),
        check_vma=False,
    )
```

```python
import functools
import math

import jax
import jax.numpy as jnp
import ml_dtypes
import numpy as np
from jax import lax
from jax.experimental import pallas as pl
from jax.experimental.pallas import tpu as pltpu
from jax.sharding import PartitionSpec as P

GRID = 48
HALF = GRID // 2 + 1
PLANE = GRID * GRID
CHUNK = 256
CHUNKS = -(-GRID * HALF // CHUNK)
TILE = 256
LANES = 128
WIDE = 2 * TILE
MESH = pl.DeviceIdType.MESH
TABLE_SCALE = 1.622
TABLE_GAIN = 1.6242055647


def plane_table():
    line = np.arange(GRID)
    k2, k3 = np.meshgrid(line, np.arange(HALF), indexing="ij")
    k2, k3 = k2.reshape(-1), k3.reshape(-1)
    b, e = np.meshgrid(line, line, indexing="ij")
    b, e = b.reshape(-1), e.reshape(-1)
    turn = (b[:, None] * k2[None] + e[:, None] * k3[None]) % GRID
    angle = 2.0 * np.pi * line / GRID
    parts = []
    for values in (np.cos(angle), -np.sin(angle)):
        small = (values * TABLE_SCALE).astype(np.float32).astype(ml_dtypes.bfloat16)
        full = np.zeros((PLANE, CHUNKS * CHUNK), ml_dtypes.bfloat16)
        full[:, : GRID * HALF] = small[turn]
        parts.append(full)
    return np.concatenate(parts, 1).reshape(PLANE, CHUNKS, WIDE).transpose(1, 0, 2)


def phase_table(val_count):
    line = np.arange(GRID)
    angle = 2.0 * np.pi * (line[:, None] * line[None] % GRID) / GRID
    scale = GRID ** (-1.5) / TABLE_GAIN
    both = np.concatenate([np.cos(angle), np.sin(angle)], 0).astype(np.float64) * scale
    both = np.repeat(both, val_count, 0).astype(np.float32)
    high = both.astype(ml_dtypes.bfloat16)
    low = (both - high.astype(np.float32)).astype(ml_dtypes.bfloat16)
    table = np.zeros((both.shape[0], LANES), ml_dtypes.bfloat16)
    table[:, :GRID] = high
    table[:, LANES // 2 : LANES // 2 + GRID] = low
    return table


def kernel(
    sizes, val_hbm, cond_hbm, table_hbm, phase_hbm, index_hbm, val_energy_hbm, cond_energy_hbm, frequencies_hbm,
    first_band_hbm, out_ref, val_ref, cond_ref, table_ref, phase_ref, index_ref, val_energy, cond_energy,
    frequencies, first_band, pair, planes, tiles, from_line, rows_in, cols_in,
    load, table_load, line_send, line_recv, plane_send, plane_recv,
):
    band_count, grow_count, gcol_count = sizes
    plane_count = band_count * gcol_count
    devices = plane_count * grow_count
    val_count = val_ref.shape[0]
    rows = val_count * GRID
    num_tiles = tiles.shape[0]
    col_tiles = num_tiles // gcol_count
    freq_count = out_ref.shape[0]
    band, grow, gcol = (lax.axis_index(name) for name in ("band", "grow", "gcol"))
    barrier = pltpu.get_barrier_semaphore()

    loads = [pltpu.make_async_copy(val_hbm, val_ref, load.at[0]), pltpu.make_async_copy(cond_hbm, cond_ref, load.at[1])]
    table_loads = [
        pltpu.make_async_copy(table_hbm.at[n], table_ref.at[n], table_load.at[n]) for n in range(CHUNKS)
    ]
    small_loads = [
        pltpu.make_async_copy(source, target, load.at[2 + n])
        for n, (source, target) in enumerate((
            (phase_hbm, phase_ref), (index_hbm, index_ref), (val_energy_hbm, val_energy),
            (cond_energy_hbm, cond_energy), (frequencies_hbm, frequencies), (first_band_hbm, first_band),
        ))
    ]
    for copy in loads + small_loads:
        copy.start()

    def turned(place, offset, count):
        place = place + offset
        return jnp.where(place >= count, place - count, place)

    def line_peer(offset):
        return band, turned(grow, offset, grow_count), gcol

    gcols = [turned(gcol, offset, gcol_count) for offset in range(gcol_count)]

    def each_plane_peer(body):
        def one_band(offset, first):
            to_band = turned(band, offset, band_count) if not first else band
            for gcol_offset in range(1 if first else 0, gcol_count):
                body((to_band, grow, gcols[gcol_offset]))

        one_band(0, True)
        if band_count <= 2:
            for offset in range(1, band_count):
                one_band(offset, False)
        else:
            pl.loop(1, band_count)(lambda offset: one_band(offset, False))

    def number_of(place):
        return (place[0] * grow_count + place[1]) * gcol_count + place[2]

    def row_tile(place):
        return (place[1] * band_count + place[0]) * num_tiles // (grow_count * band_count)

    def greet(place):
        pl.semaphore_signal(barrier, inc=1, device_id=place, device_id_type=MESH)

    for offset in range(1, grow_count):
        greet(line_peer(offset))
    each_plane_peer(greet)

    for copy in loads:
        copy.wait()
    for copy in table_loads:
        copy.start()
    group = 16 // val_count

    @pl.loop(0, GRID // group)
    def _(block):
        products = []
        for member in range(group):
            where = pl.ds(pl.multiple_of((block * group + member) * PLANE, LANES), PLANE)
            products.append(val_ref[:, where].astype(jnp.float32) * cond_ref[:, where].astype(jnp.float32))
        product = jnp.concatenate(products, 0)
        high = product.astype(jnp.bfloat16)
        start = pl.multiple_of(block * 16, 16)
        pair[pl.ds(start, 16)] = high
        pair[pl.ds(rows + start, 16)] = (product - high.astype(jnp.float32)).astype(jnp.bfloat16)

    for step in range(CHUNKS):
        table_loads[step].wait()
        both = jnp.dot(pair[...], table_ref[step], preferred_element_type=jnp.float32)
        total = (both[:rows] + both[rows:]).astype(jnp.bfloat16)
        for side in range(2):
            number = 2 * step + side
            start = number // CHUNKS * rows
            planes[start : start + rows, pl.ds(number % CHUNKS * CHUNK, CHUNK)] = (
                total[:, side * CHUNK : (side + 1) * CHUNK]
            )

    for copy in small_loads:
        copy.wait()
    pl.semaphore_wait(barrier, grow_count - 1 + plane_count - 1)

    @pl.loop(0, num_tiles // 2)
    def _(tile):
        index = index_ref[tile]
        index_float = index.astype(jnp.float32)
        upper = jnp.floor((index_float + 0.5) * (1.0 / GRID))
        k3 = index_float - GRID * upper
        k1 = jnp.floor((upper + 0.5) * (1.0 / GRID))
        k2 = upper - GRID * k1
        mirror = k3 > HALF - 1
        k1 = jnp.where(mirror & (k1 > 0), GRID - k1, k1).astype(jnp.int32)
        k2 = jnp.where(mirror & (k2 > 0), GRID - k2, k2)
        k3 = jnp.where(mirror, GRID - k3, k3)
        sign = jnp.where(mirror, -1.0, 1.0)
        place = (k2 * HALF + k3).astype(jnp.int32)
        line = lax.broadcasted_iota(jnp.int32, (CHUNKS * CHUNK, WIDE), 0)
        pick = jnp.where(line == place, 1.0, 0.0).astype(jnp.bfloat16)
        picked = jnp.dot(planes[...], pick, preferred_element_type=jnp.float32)
        real, imag = picked[:rows], picked[rows:]
        line = line[:LANES]
        pick = jnp.where((line == k1) | (line == k1 + LANES // 2), 1.0, 0.0).astype(jnp.bfloat16)
        phases = jnp.dot(phase_ref[...], pick, preferred_element_type=jnp.float32)
        cos_one, sin_one = phases[:rows], phases[rows:]
        out = []
        for value, flip in (
            (real * cos_one + imag * sin_one, None),
            (imag * cos_one - real * sin_one, sign),
        ):
            value = jnp.sum(value.reshape(rows // 8, 8, WIDE), axis=0)
            value = sum(value[n * val_count : (n + 1) * val_count] for n in range(8 // val_count))
            out.append(value if flip is None else value * flip)
        out = jnp.concatenate(out, 0)
        out = [out[:, n * LANES : (n + 1) * LANES] for n in range(WIDE // LANES)]
        for side in range(2):
            tiles[2 * tile + side] = jnp.concatenate(out[2 * side : 2 * side + 2], 0).astype(jnp.bfloat16)
        for offset in range(1, grow_count):
            pltpu.make_async_remote_copy(
                tiles.at[pl.ds(2 * tile, 2)], from_line.at[offset - 1, pl.ds(2 * tile, 2)], line_send, line_recv.at[offset - 1],
                device_id=line_peer(offset), device_id_type=MESH,
            ).start()

    def spread(source, origin):
        def send(place):
            pltpu.make_async_remote_copy(
                source.at[row_tile(place)], rows_in.at[origin], plane_send.at[0], plane_recv.at[0],
                device_id=place, device_id_type=MESH,
            ).start()
            pltpu.make_async_remote_copy(
                source.at[pl.ds(place[2] * col_tiles, col_tiles)], cols_in.at[origin],
                plane_send.at[1], plane_recv.at[1],
                device_id=place, device_id_type=MESH,
            ).start()

        each_plane_peer(send)
        place = (band, grow, gcol)
        pltpu.make_async_copy(source.at[row_tile(place)], rows_in.at[origin], plane_recv.at[0]).start()
        pltpu.make_async_copy(
            source.at[pl.ds(gcol * col_tiles, col_tiles)], cols_in.at[origin], plane_recv.at[1]
        ).start()

    spread(tiles, number_of((band, grow, gcol)))
    for offset in range(1, grow_count):
        arrived = from_line.at[offset - 1]
        pltpu.make_async_copy(arrived, arrived, line_recv.at[offset - 1]).wait()
        spread(arrived, number_of(line_peer(grow_count - offset)))

    half = 2 * val_count
    depth = devices * half
    row = lax.broadcasted_iota(jnp.int32, (depth, 1), 0)

    def along_rows(values, number):
        lane = lax.broadcasted_iota(jnp.int32, (depth, values.shape[1]), 1)
        return jnp.sum(jnp.where(lane == number, values, 0), axis=1, keepdims=True)

    band_id = row // half
    val_id = row % val_count
    gap = along_rows(cond_energy[...], band_id) - along_rows(val_energy[...], val_id)
    counted = band_id >= along_rows(first_band[...], val_id)
    weights = []
    for freq in range(freq_count):
        denominator = gap * gap + frequencies[:, freq : freq + 1] * frequencies[:, freq : freq + 1]
        weights.append(jnp.where(counted, -4.0 * gap / denominator, 0.0) / (devices * val_count))

    pltpu.make_async_copy(rows_in, rows_in, plane_recv.at[0]).wait()
    pltpu.make_async_copy(cols_in, cols_in, plane_recv.at[1]).wait()

    cols = cols_in[...].astype(jnp.float32)
    right = jnp.concatenate(
        [cols[:, tile, side * half : (side + 1) * half].reshape(depth, LANES)
         for tile in range(col_tiles) for side in range(2)], 1
    ).astype(jnp.bfloat16)
    inward = rows_in[...].astype(jnp.float32)
    parts = [inward[:, side * half : (side + 1) * half].reshape(depth, LANES) for side in range(2)]
    lefts = []
    for freq in range(freq_count):
        kept = [part * weights[freq] for part in parts]
        cubes = [left.reshape(devices, half, LANES) for left in kept]
        turned_round = [
            jnp.concatenate([cube[:, val_count:], -cube[:, :val_count]], 1).reshape(depth, LANES) for cube in cubes
        ]
        lefts += kept + turned_round
    left = jnp.concatenate(lefts, 1).astype(jnp.bfloat16)
    out_ref[...] = lax.dot_general(
        left, right, (((0,), (0,)), ((), ())), preferred_element_type=jnp.float32
    ).astype(jnp.bfloat16).reshape(out_ref.shape)

    pltpu.make_async_copy(from_line, from_line, line_send).wait()
    for held, sem in ((rows_in, 0), (cols_in, 1)):
        sent = held.at[pl.ds(0, (plane_count - 1) * grow_count)]
        pltpu.make_async_copy(sent, sent, plane_send.at[sem]).wait()


def on_device(sizes, valence, conduction, val_energy, cond_energy, frequencies, gvec_index, first_band):
    band_count, grow_count, gcol_count = sizes
    devices = band_count * grow_count * gcol_count
    val_count = val_energy.shape[0]
    freq_count = frequencies.shape[0]
    num_gvec = gvec_index.shape[0]
    rows = val_count * GRID
    num_tiles = num_gvec // TILE
    col_tiles = num_tiles // gcol_count
    tile_shape = (4 * val_count, LANES)
    operands = (
        valence,
        conduction,
        jnp.asarray(plane_table()),
        jnp.asarray(phase_table(val_count)),
        gvec_index.reshape(num_tiles // 2, 1, WIDE),
        val_energy[None],
        cond_energy[None],
        frequencies[None],
        first_band[None],
    )
    out_shape = (freq_count, 2, TILE, num_gvec // gcol_count)
    out = pl.pallas_call(
        functools.partial(kernel, sizes),
        out_shape=jax.ShapeDtypeStruct(out_shape, jnp.bfloat16),
        in_specs=[pl.BlockSpec(memory_space=pl.ANY)] * len(operands),
        out_specs=pl.BlockSpec(memory_space=pltpu.VMEM),
        scratch_shapes=[
            pltpu.VMEM(valence.shape, jnp.bfloat16),
            pltpu.VMEM(conduction.shape, jnp.bfloat16),
            pltpu.VMEM((CHUNKS, PLANE, WIDE), jnp.bfloat16),
            *(pltpu.VMEM(operand.shape, operand.dtype) for operand in operands[3:]),
            pltpu.VMEM((2 * rows, PLANE), jnp.bfloat16),
            pltpu.VMEM((2 * rows, CHUNKS * CHUNK), jnp.bfloat16),
            pltpu.VMEM((num_tiles,) + tile_shape, jnp.bfloat16),
            pltpu.VMEM((grow_count - 1, num_tiles) + tile_shape, jnp.bfloat16),
            pltpu.VMEM((devices,) + tile_shape, jnp.bfloat16),
            pltpu.VMEM((devices, col_tiles) + tile_shape, jnp.bfloat16),
            pltpu.SemaphoreType.DMA((len(operands) - 1,)),
            pltpu.SemaphoreType.DMA((CHUNKS,)),
            pltpu.SemaphoreType.DMA,
            pltpu.SemaphoreType.DMA((grow_count - 1,)),
            pltpu.SemaphoreType.DMA((2,)),
            pltpu.SemaphoreType.DMA((2,)),
        ],
        compiler_params=pltpu.CompilerParams(
            collective_id=0, has_side_effects=True, vmem_limit_bytes=63 * 2**20
        ),
    )(*operands)
    out = jnp.transpose(out, (2, 0, 1, 3))
    row_count = num_gvec // (grow_count * band_count)
    if row_count < TILE:
        block = lax.axis_index("grow") * band_count + lax.axis_index("band")
        out = lax.dynamic_slice_in_dim(out, block * row_count % TILE, row_count, 0)
    return out


def solution(mesh):
    sizes = tuple(mesh.shape[name] for name in ("band", "grow", "gcol"))
    return jax.shard_map(
        functools.partial(on_device, sizes),
        mesh=mesh,
        in_specs=(P(), P(("band", "grow", "gcol"), None), P(), P(), P(), P(), P()),
        out_specs=P(("grow", "band"), None, None, "gcol"),
        check_vma=False,
    )
```

```python
import functools
import math

import jax
import jax.numpy as jnp
import ml_dtypes
import numpy as np
from jax import lax
from jax.experimental import pallas as pl
from jax.experimental.pallas import tpu as pltpu
from jax.sharding import PartitionSpec as P

GRID = 48
HALF = GRID // 2 + 1
PLANE = GRID * GRID
CHUNK = 256
CHUNKS = -(-GRID * HALF // CHUNK)
TILE = 256
LANES = 128
WIDE = 2 * TILE
MESH = pl.DeviceIdType.MESH
TABLE_SCALE = 1.622
TABLE_GAIN = 1.6242055647


def plane_table():
    line = np.arange(GRID)
    k2, k3 = np.meshgrid(line, np.arange(HALF), indexing="ij")
    k2, k3 = k2.reshape(-1), k3.reshape(-1)
    b, e = np.meshgrid(line, line, indexing="ij")
    b, e = b.reshape(-1), e.reshape(-1)
    turn = (b[:, None] * k2[None] + e[:, None] * k3[None]) % GRID
    angle = 2.0 * np.pi * line / GRID
    parts = []
    for values in (np.cos(angle), -np.sin(angle)):
        small = (values * TABLE_SCALE).astype(np.float32).astype(ml_dtypes.bfloat16)
        full = np.zeros((PLANE, CHUNKS * CHUNK), ml_dtypes.bfloat16)
        full[:, : GRID * HALF] = small[turn]
        parts.append(full)
    return np.concatenate(parts, 1).reshape(PLANE, CHUNKS, WIDE).transpose(1, 0, 2)


def phase_table(val_count):
    line = np.arange(GRID)
    angle = 2.0 * np.pi * (line[:, None] * line[None] % GRID) / GRID
    scale = GRID ** (-1.5) / TABLE_GAIN
    both = np.concatenate([np.cos(angle), np.sin(angle)], 0).astype(np.float64) * scale
    both = np.repeat(both, val_count, 0).astype(np.float32)
    high = both.astype(ml_dtypes.bfloat16)
    low = (both - high.astype(np.float32)).astype(ml_dtypes.bfloat16)
    table = np.zeros((both.shape[0], LANES), ml_dtypes.bfloat16)
    table[:, :GRID] = high
    table[:, LANES // 2 : LANES // 2 + GRID] = low
    return table


def kernel(
    sizes, val_hbm, cond_hbm, table_hbm, phase_hbm, index_hbm, val_energy_hbm, cond_energy_hbm, frequencies_hbm,
    first_band_hbm, out_ref, val_ref, cond_ref, table_ref, phase_ref, index_ref, val_energy, cond_energy,
    frequencies, first_band, pair, planes, tiles, from_line, rows_in, cols_in,
    load, table_load, line_send, line_recv, plane_send, plane_recv,
):
    band_count, grow_count, gcol_count = sizes
    plane_count = band_count * gcol_count
    devices = plane_count * grow_count
    val_count = val_ref.shape[0]
    rows = val_count * GRID
    num_tiles = tiles.shape[0]
    col_tiles = num_tiles // gcol_count
    freq_count = frequencies.shape[1]
    band, grow, gcol = (lax.axis_index(name) for name in ("band", "grow", "gcol"))
    barrier = pltpu.get_barrier_semaphore()

    loads = [pltpu.make_async_copy(val_hbm, val_ref, load.at[0]), pltpu.make_async_copy(cond_hbm, cond_ref, load.at[1])]
    table_loads = [
        pltpu.make_async_copy(table_hbm.at[n], table_ref.at[n], table_load.at[n]) for n in range(CHUNKS)
    ]
    small_loads = [
        pltpu.make_async_copy(source, target, load.at[2 + n])
        for n, (source, target) in enumerate((
            (phase_hbm, phase_ref), (index_hbm, index_ref), (val_energy_hbm, val_energy),
            (cond_energy_hbm, cond_energy), (frequencies_hbm, frequencies), (first_band_hbm, first_band),
        ))
    ]
    for copy in loads + small_loads:
        copy.start()

    def turned(place, offset, count):
        place = place + offset
        return jnp.where(place >= count, place - count, place)

    def line_peer(offset):
        return band, turned(grow, offset, grow_count), gcol

    gcols = [turned(gcol, offset, gcol_count) for offset in range(gcol_count)]

    def each_plane_peer(body):
        def one_band(offset, first):
            to_band = turned(band, offset, band_count) if not first else band
            for gcol_offset in range(1 if first else 0, gcol_count):
                body((to_band, grow, gcols[gcol_offset]))

        one_band(0, True)
        if band_count <= 2:
            for offset in range(1, band_count):
                one_band(offset, False)
        else:
            pl.loop(1, band_count)(lambda offset: one_band(offset, False))

    def number_of(place):
        return (place[0] * grow_count + place[1]) * gcol_count + place[2]

    def row_tile(place):
        return (place[1] * band_count + place[0]) * num_tiles // (grow_count * band_count)

    def greet(place):
        pl.semaphore_signal(barrier, inc=1, device_id=place, device_id_type=MESH)

    for offset in range(1, grow_count):
        greet(line_peer(offset))
    each_plane_peer(greet)

    for copy in loads:
        copy.wait()
    for copy in table_loads:
        copy.start()
    group = 16 // val_count

    @pl.loop(0, GRID // group)
    def _(block):
        products = []
        for member in range(group):
            where = pl.ds(pl.multiple_of((block * group + member) * PLANE, LANES), PLANE)
            products.append(val_ref[:, where].astype(jnp.float32) * cond_ref[:, where].astype(jnp.float32))
        product = jnp.concatenate(products, 0)
        high = product.astype(jnp.bfloat16)
        start = pl.multiple_of(block * 16, 16)
        pair[pl.ds(start, 16)] = high
        pair[pl.ds(rows + start, 16)] = (product - high.astype(jnp.float32)).astype(jnp.bfloat16)

    for step in range(CHUNKS):
        table_loads[step].wait()
        both = jnp.dot(pair[...], table_ref[step], preferred_element_type=jnp.float32)
        total = (both[:rows] + both[rows:]).astype(jnp.bfloat16)
        for side in range(2):
            number = 2 * step + side
            start = number // CHUNKS * rows
            planes[start : start + rows, pl.ds(number % CHUNKS * CHUNK, CHUNK)] = (
                total[:, side * CHUNK : (side + 1) * CHUNK]
            )

    for copy in small_loads:
        copy.wait()
    pl.semaphore_wait(barrier, grow_count - 1 + plane_count - 1)

    @pl.loop(0, num_tiles // 2)
    def _(tile):
        index = index_ref[tile]
        index_float = index.astype(jnp.float32)
        upper = jnp.floor((index_float + 0.5) * (1.0 / GRID))
        k3 = index_float - GRID * upper
        k1 = jnp.floor((upper + 0.5) * (1.0 / GRID))
        k2 = upper - GRID * k1
        mirror = k3 > HALF - 1
        k1 = jnp.where(mirror & (k1 > 0), GRID - k1, k1).astype(jnp.int32)
        k2 = jnp.where(mirror & (k2 > 0), GRID - k2, k2)
        k3 = jnp.where(mirror, GRID - k3, k3)
        sign = jnp.where(mirror, -1.0, 1.0)
        place = (k2 * HALF + k3).astype(jnp.int32)
        line = lax.broadcasted_iota(jnp.int32, (CHUNKS * CHUNK, WIDE), 0)
        pick = jnp.where(line == place, 1.0, 0.0).astype(jnp.bfloat16)
        picked = jnp.dot(planes[...], pick, preferred_element_type=jnp.float32)
        real, imag = picked[:rows], picked[rows:]
        line = line[:LANES]
        pick = jnp.where((line == k1) | (line == k1 + LANES // 2), 1.0, 0.0).astype(jnp.bfloat16)
        phases = jnp.dot(phase_ref[...], pick, preferred_element_type=jnp.float32)
        cos_one, sin_one = phases[:rows], phases[rows:]
        out = []
        for value, flip in (
            (real * cos_one + imag * sin_one, None),
            (imag * cos_one - real * sin_one, sign),
        ):
            value = jnp.sum(value.reshape(rows // 8, 8, WIDE), axis=0)
            value = sum(value[n * val_count : (n + 1) * val_count] for n in range(8 // val_count))
            out.append(value if flip is None else value * flip)
        out = jnp.concatenate(out, 0)
        out = [out[:, n * LANES : (n + 1) * LANES] for n in range(WIDE // LANES)]
        for side in range(2):
            tiles[2 * tile + side] = jnp.concatenate(out[2 * side : 2 * side + 2], 0).astype(jnp.bfloat16)
        for offset in range(1, grow_count):
            pltpu.make_async_remote_copy(
                tiles.at[pl.ds(2 * tile, 2)], from_line.at[offset - 1, pl.ds(2 * tile, 2)], line_send, line_recv.at[offset - 1],
                device_id=line_peer(offset), device_id_type=MESH,
            ).start()

    def spread(source, origin):
        def send(place):
            pltpu.make_async_remote_copy(
                source.at[row_tile(place)], rows_in.at[origin], plane_send.at[0], plane_recv.at[0],
                device_id=place, device_id_type=MESH,
            ).start()
            pltpu.make_async_remote_copy(
                source.at[pl.ds(place[2] * col_tiles, col_tiles)], cols_in.at[origin],
                plane_send.at[1], plane_recv.at[1],
                device_id=place, device_id_type=MESH,
            ).start()

        each_plane_peer(send)
        place = (band, grow, gcol)
        pltpu.make_async_copy(source.at[row_tile(place)], rows_in.at[origin], plane_recv.at[0]).start()
        pltpu.make_async_copy(
            source.at[pl.ds(gcol * col_tiles, col_tiles)], cols_in.at[origin], plane_recv.at[1]
        ).start()

    spread(tiles, number_of((band, grow, gcol)))
    for offset in range(1, grow_count):
        arrived = from_line.at[offset - 1]
        pltpu.make_async_copy(arrived, arrived, line_recv.at[offset - 1]).wait()
        spread(arrived, number_of(line_peer(grow_count - offset)))

    half = 2 * val_count
    depth = devices * half
    row = lax.broadcasted_iota(jnp.int32, (depth, 1), 0)

    def along_rows(values, number):
        lane = lax.broadcasted_iota(jnp.int32, (depth, values.shape[1]), 1)
        return jnp.sum(jnp.where(lane == number, values, 0), axis=1, keepdims=True)

    band_id = row // half
    val_id = row % val_count
    gap = along_rows(cond_energy[...], band_id) - along_rows(val_energy[...], val_id)
    counted = band_id >= along_rows(first_band[...], val_id)
    weights = []
    for freq in range(freq_count):
        denominator = gap * gap + frequencies[:, freq : freq + 1] * frequencies[:, freq : freq + 1]
        weights.append(jnp.where(counted, -4.0 * gap / denominator, 0.0) / (devices * val_count))

    pltpu.make_async_copy(rows_in, rows_in, plane_recv.at[0]).wait()
    pltpu.make_async_copy(cols_in, cols_in, plane_recv.at[1]).wait()

    cols = cols_in[...].astype(jnp.float32)
    right = jnp.concatenate(
        [cols[:, tile, side * half : (side + 1) * half].reshape(depth, LANES)
         for tile in range(col_tiles) for side in range(2)], 1
    ).astype(jnp.bfloat16)
    inward = rows_in[...].astype(jnp.float32)
    inward = jnp.concatenate(
        [inward[:, side * half : (side + 1) * half].reshape(depth, LANES) for side in range(2)], 1
    ).astype(jnp.bfloat16)
    wide = out_ref.shape[0]
    copies = wide // TILE
    lane = lax.broadcasted_iota(jnp.int32, (TILE, wide), 1)
    repeat = jnp.where(lane // copies == lax.broadcasted_iota(jnp.int32, (TILE, wide), 0), 1.0, 0.0)
    left = jnp.dot(inward, repeat.astype(jnp.bfloat16), preferred_element_type=jnp.float32)
    lane = lax.broadcasted_iota(jnp.int32, (1, wide), 1)
    weight = weights[0]
    for freq in range(1, freq_count):
        weight = jnp.where(lane // 2 % freq_count == freq, weights[freq], weight)
    cube = (left * weight).reshape(devices, half, wide)
    swapped = jnp.concatenate([cube[:, val_count:], -cube[:, :val_count]], 1)
    left = jnp.where((lane % 2 == 1)[None], swapped, cube).reshape(depth, wide).astype(jnp.bfloat16)
    out_ref[...] = lax.dot_general(
        left, right, (((0,), (0,)), ((), ())), preferred_element_type=jnp.float32
    ).astype(jnp.bfloat16)

    pltpu.make_async_copy(from_line, from_line, line_send).wait()
    for held, sem in ((rows_in, 0), (cols_in, 1)):
        sent = held.at[pl.ds(0, (plane_count - 1) * grow_count)]
        pltpu.make_async_copy(sent, sent, plane_send.at[sem]).wait()


def on_device(sizes, valence, conduction, val_energy, cond_energy, frequencies, gvec_index, first_band):
    band_count, grow_count, gcol_count = sizes
    devices = band_count * grow_count * gcol_count
    val_count = val_energy.shape[0]
    freq_count = frequencies.shape[0]
    num_gvec = gvec_index.shape[0]
    rows = val_count * GRID
    num_tiles = num_gvec // TILE
    col_tiles = num_tiles // gcol_count
    tile_shape = (4 * val_count, LANES)
    operands = (
        valence,
        conduction,
        jnp.asarray(plane_table()),
        jnp.asarray(phase_table(val_count)),
        gvec_index.reshape(num_tiles // 2, 1, WIDE),
        val_energy[None],
        cond_energy[None],
        frequencies[None],
        first_band[None],
    )
    out_shape = (TILE * freq_count * 2, num_gvec // gcol_count)
    out = pl.pallas_call(
        functools.partial(kernel, sizes),
        out_shape=jax.ShapeDtypeStruct(out_shape, jnp.bfloat16),
        in_specs=[pl.BlockSpec(memory_space=pl.ANY)] * len(operands),
        out_specs=pl.BlockSpec(memory_space=pltpu.VMEM),
        scratch_shapes=[
            pltpu.VMEM(valence.shape, jnp.bfloat16),
            pltpu.VMEM(conduction.shape, jnp.bfloat16),
            pltpu.VMEM((CHUNKS, PLANE, WIDE), jnp.bfloat16),
            *(pltpu.VMEM(operand.shape, operand.dtype) for operand in operands[3:]),
            pltpu.VMEM((2 * rows, PLANE), jnp.bfloat16),
            pltpu.VMEM((2 * rows, CHUNKS * CHUNK), jnp.bfloat16),
            pltpu.VMEM((num_tiles,) + tile_shape, jnp.bfloat16),
            pltpu.VMEM((grow_count - 1, num_tiles) + tile_shape, jnp.bfloat16),
            pltpu.VMEM((devices,) + tile_shape, jnp.bfloat16),
            pltpu.VMEM((devices, col_tiles) + tile_shape, jnp.bfloat16),
            pltpu.SemaphoreType.DMA((len(operands) - 1,)),
            pltpu.SemaphoreType.DMA((CHUNKS,)),
            pltpu.SemaphoreType.DMA,
            pltpu.SemaphoreType.DMA((grow_count - 1,)),
            pltpu.SemaphoreType.DMA((2,)),
            pltpu.SemaphoreType.DMA((2,)),
        ],
        compiler_params=pltpu.CompilerParams(
            collective_id=0, has_side_effects=True, vmem_limit_bytes=63 * 2**20
        ),
    )(*operands)
    out = out.reshape(TILE, freq_count, 2, num_gvec // gcol_count)
    row_count = num_gvec // (grow_count * band_count)
    if row_count < TILE:
        block = lax.axis_index("grow") * band_count + lax.axis_index("band")
        out = lax.dynamic_slice_in_dim(out, block * row_count % TILE, row_count, 0)
    return out


def solution(mesh):
    sizes = tuple(mesh.shape[name] for name in ("band", "grow", "gcol"))
    return jax.shard_map(
        functools.partial(on_device, sizes),
        mesh=mesh,
        in_specs=(P(), P(("band", "grow", "gcol"), None), P(), P(), P(), P(), P()),
        out_specs=P(("grow", "band"), None, None, "gcol"),
        check_vma=False,
    )
```

```python
import functools
import math

import jax
import jax.numpy as jnp
import ml_dtypes
import numpy as np
from jax import lax
from jax.experimental import pallas as pl
from jax.experimental.pallas import tpu as pltpu
from jax.sharding import PartitionSpec as P

GRID = 48
HALF = GRID // 2 + 1
PLANE = GRID * GRID
CHUNK = 256
CHUNKS = -(-GRID * HALF // CHUNK)
TILE = 256
LANES = 128
WIDE = 2 * TILE
MESH = pl.DeviceIdType.MESH
TABLE_SCALE = 1.622
TABLE_GAIN = 1.6242055647


def plane_table():
    line = np.arange(GRID)
    k2, k3 = np.meshgrid(line, np.arange(HALF), indexing="ij")
    k2, k3 = k2.reshape(-1), k3.reshape(-1)
    b, e = np.meshgrid(line, line, indexing="ij")
    b, e = b.reshape(-1), e.reshape(-1)
    turn = (b[:, None] * k2[None] + e[:, None] * k3[None]) % GRID
    angle = 2.0 * np.pi * line / GRID
    parts = []
    for values in (np.cos(angle), -np.sin(angle)):
        small = (values * TABLE_SCALE).astype(np.float32).astype(ml_dtypes.bfloat16)
        full = np.zeros((PLANE, CHUNKS * CHUNK), ml_dtypes.bfloat16)
        full[:, : GRID * HALF] = small[turn]
        parts.append(full)
    return np.concatenate(parts, 1).reshape(PLANE, CHUNKS, WIDE).transpose(1, 0, 2)


def phase_table(val_count):
    line = np.arange(GRID)
    angle = 2.0 * np.pi * (line[:, None] * line[None] % GRID) / GRID
    scale = GRID ** (-1.5) / TABLE_GAIN
    both = np.concatenate([np.cos(angle), np.sin(angle)], 0).astype(np.float64) * scale
    both = np.repeat(both, val_count, 0).astype(np.float32)
    high = both.astype(ml_dtypes.bfloat16)
    low = (both - high.astype(np.float32)).astype(ml_dtypes.bfloat16)
    table = np.zeros((both.shape[0], LANES), ml_dtypes.bfloat16)
    table[:, :GRID] = high
    table[:, LANES // 2 : LANES // 2 + GRID] = low
    return table


def kernel(
    sizes, val_hbm, cond_hbm, table_hbm, phase_hbm, index_hbm, val_energy_hbm, cond_energy_hbm, frequencies_hbm,
    first_band_hbm, out_ref, val_ref, cond_ref, table_ref, phase_ref, index_ref, val_energy, cond_energy,
    frequencies, first_band, pair, planes, tiles, from_line, rows_in, cols_in,
    load, table_load, line_send, line_recv, plane_send, plane_recv,
):
    band_count, grow_count, gcol_count = sizes
    plane_count = band_count * gcol_count
    devices = plane_count * grow_count
    val_count = val_ref.shape[0]
    rows = val_count * GRID
    num_tiles = tiles.shape[0]
    col_tiles = num_tiles // gcol_count
    freq_count = frequencies.shape[1]
    band, grow, gcol = (lax.axis_index(name) for name in ("band", "grow", "gcol"))
    barrier = pltpu.get_barrier_semaphore()

    loads = [pltpu.make_async_copy(val_hbm, val_ref, load.at[0]), pltpu.make_async_copy(cond_hbm, cond_ref, load.at[1])]
    table_loads = [
        pltpu.make_async_copy(table_hbm.at[n], table_ref.at[n], table_load.at[n]) for n in range(CHUNKS)
    ]
    small_loads = [
        pltpu.make_async_copy(source, target, load.at[2 + n])
        for n, (source, target) in enumerate((
            (phase_hbm, phase_ref), (index_hbm, index_ref), (val_energy_hbm, val_energy),
            (cond_energy_hbm, cond_energy), (frequencies_hbm, frequencies), (first_band_hbm, first_band),
        ))
    ]
    for copy in loads + small_loads:
        copy.start()

    def turned(place, offset, count):
        place = place + offset
        return jnp.where(place >= count, place - count, place)

    def line_peer(offset):
        return band, turned(grow, offset, grow_count), gcol

    gcols = [turned(gcol, offset, gcol_count) for offset in range(gcol_count)]

    def each_plane_peer(body):
        def one_band(offset, first):
            to_band = turned(band, offset, band_count) if not first else band
            for gcol_offset in range(1 if first else 0, gcol_count):
                body((to_band, grow, gcols[gcol_offset]))

        one_band(0, True)
        if band_count <= 2:
            for offset in range(1, band_count):
                one_band(offset, False)
        else:
            pl.loop(1, band_count)(lambda offset: one_band(offset, False))

    def number_of(place):
        return (place[0] * grow_count + place[1]) * gcol_count + place[2]

    def row_tile(place):
        return (place[1] * band_count + place[0]) * num_tiles // (grow_count * band_count)

    def greet(place):
        pl.semaphore_signal(barrier, inc=1, device_id=place, device_id_type=MESH)

    for offset in range(1, grow_count):
        greet(line_peer(offset))
    each_plane_peer(greet)

    for copy in loads:
        copy.wait()
    for copy in table_loads:
        copy.start()
    group = 16 // val_count

    @pl.loop(0, GRID // group)
    def _(block):
        products = []
        for member in range(group):
            where = pl.ds(pl.multiple_of((block * group + member) * PLANE, LANES), PLANE)
            products.append(val_ref[:, where].astype(jnp.float32) * cond_ref[:, where].astype(jnp.float32))
        product = jnp.concatenate(products, 0)
        high = product.astype(jnp.bfloat16)
        start = pl.multiple_of(block * 16, 16)
        pair[pl.ds(start, 16)] = high
        pair[pl.ds(rows + start, 16)] = (product - high.astype(jnp.float32)).astype(jnp.bfloat16)

    for step in range(CHUNKS):
        table_loads[step].wait()
        both = jnp.dot(pair[...], table_ref[step], preferred_element_type=jnp.float32)
        total = (both[:rows] + both[rows:]).astype(jnp.bfloat16)
        for side in range(2):
            number = 2 * step + side
            start = number // CHUNKS * rows
            planes[start : start + rows, pl.ds(number % CHUNKS * CHUNK, CHUNK)] = (
                total[:, side * CHUNK : (side + 1) * CHUNK]
            )

    for copy in small_loads:
        copy.wait()
    pl.semaphore_wait(barrier, grow_count - 1 + plane_count - 1)

    here = (band, grow, gcol)
    pair_count = num_tiles // 2

    def send(source, target, sem, place):
        pltpu.make_async_remote_copy(
            source, target, plane_send.at[sem], plane_recv.at[sem], device_id=place, device_id_type=MESH
        ).start()

    def spread(source, origin, number):
        columns = source.at[pl.ds(number * col_tiles, col_tiles)]

        @pl.when(number == gcol)
        def _():
            pltpu.make_async_copy(columns, cols_in.at[origin], plane_recv.at[1]).start()

        @pl.when(number != gcol)
        def _():
            send(columns, cols_in.at[origin], 1, (band, grow, number))

        for offset in range(1, band_count):
            send(columns, cols_in.at[origin], 1, (turned(band, offset, band_count), grow, number))

        @pl.when(number == grow)
        def _():
            pltpu.make_async_copy(source.at[row_tile(here)], rows_in.at[origin], plane_recv.at[0]).start()
            each_plane_peer(lambda place: send(source.at[row_tile(place)], rows_in.at[origin], 0, place))

    def forward(number):
        for offset in range(1, grow_count):
            arrived = from_line.at[offset - 1]
            part = arrived.at[pl.ds(2 * number, 2)]
            pltpu.make_async_copy(part, part, line_recv.at[offset - 1, number]).wait()
            spread(arrived, number_of(line_peer(grow_count - offset)), number)

    @pl.loop(0, pair_count)
    def _(tile):
        index = index_ref[tile]
        index_float = index.astype(jnp.float32)
        upper = jnp.floor((index_float + 0.5) * (1.0 / GRID))
        k3 = index_float - GRID * upper
        k1 = jnp.floor((upper + 0.5) * (1.0 / GRID))
        k2 = upper - GRID * k1
        mirror = k3 > HALF - 1
        k1 = jnp.where(mirror & (k1 > 0), GRID - k1, k1).astype(jnp.int32)
        k2 = jnp.where(mirror & (k2 > 0), GRID - k2, k2)
        k3 = jnp.where(mirror, GRID - k3, k3)
        sign = jnp.where(mirror, -1.0, 1.0)
        place = (k2 * HALF + k3).astype(jnp.int32)
        line = lax.broadcasted_iota(jnp.int32, (CHUNKS * CHUNK, WIDE), 0)
        pick = jnp.where(line == place, 1.0, 0.0).astype(jnp.bfloat16)
        picked = jnp.dot(planes[...], pick, preferred_element_type=jnp.float32)
        real, imag = picked[:rows], picked[rows:]
        line = line[:LANES]
        pick = jnp.where((line == k1) | (line == k1 + LANES // 2), 1.0, 0.0).astype(jnp.bfloat16)
        phases = jnp.dot(phase_ref[...], pick, preferred_element_type=jnp.float32)
        cos_one, sin_one = phases[:rows], phases[rows:]
        out = []
        for value, flip in (
            (real * cos_one + imag * sin_one, None),
            (imag * cos_one - real * sin_one, sign),
        ):
            value = jnp.sum(value.reshape(rows // 8, 8, WIDE), axis=0)
            value = sum(value[n * val_count : (n + 1) * val_count] for n in range(8 // val_count))
            out.append(value if flip is None else value * flip)
        out = jnp.concatenate(out, 0)
        out = [out[:, n * LANES : (n + 1) * LANES] for n in range(WIDE // LANES)]
        for side in range(2):
            tiles[2 * tile + side] = jnp.concatenate(out[2 * side : 2 * side + 2], 0).astype(jnp.bfloat16)
        for offset in range(1, grow_count):
            pltpu.make_async_remote_copy(
                tiles.at[pl.ds(2 * tile, 2)], from_line.at[offset - 1, pl.ds(2 * tile, 2)], line_send, line_recv.at[offset - 1, tile],
                device_id=line_peer(offset), device_id_type=MESH,
            ).start()
        spread(tiles, number_of(here), tile)
        pl.when(tile >= 1)(lambda: forward(tile - 1))

    forward(pair_count - 1)

    half = 2 * val_count
    depth = devices * half
    row = lax.broadcasted_iota(jnp.int32, (depth, 1), 0)

    def along_rows(values, number):
        lane = lax.broadcasted_iota(jnp.int32, (depth, values.shape[1]), 1)
        return jnp.sum(jnp.where(lane == number, values, 0), axis=1, keepdims=True)

    band_id = row // half
    val_id = row % val_count
    gap = along_rows(cond_energy[...], band_id) - along_rows(val_energy[...], val_id)
    counted = band_id >= along_rows(first_band[...], val_id)
    weights = []
    for freq in range(freq_count):
        denominator = gap * gap + frequencies[:, freq : freq + 1] * frequencies[:, freq : freq + 1]
        weights.append(jnp.where(counted, -4.0 * gap / denominator, 0.0) / (devices * val_count))

    pltpu.make_async_copy(rows_in, rows_in, plane_recv.at[0]).wait()
    pltpu.make_async_copy(cols_in, cols_in, plane_recv.at[1]).wait()

    cols = cols_in[...].astype(jnp.float32)
    right = jnp.concatenate(
        [cols[:, tile, side * half : (side + 1) * half].reshape(depth, LANES)
         for tile in range(col_tiles) for side in range(2)], 1
    ).astype(jnp.bfloat16)
    inward = rows_in[...].astype(jnp.float32)
    inward = jnp.concatenate(
        [inward[:, side * half : (side + 1) * half].reshape(depth, LANES) for side in range(2)], 1
    ).astype(jnp.bfloat16)
    wide = out_ref.shape[0]
    copies = wide // TILE
    lane = lax.broadcasted_iota(jnp.int32, (TILE, wide), 1)
    repeat = jnp.where(lane // copies == lax.broadcasted_iota(jnp.int32, (TILE, wide), 0), 1.0, 0.0)
    left = jnp.dot(inward, repeat.astype(jnp.bfloat16), preferred_element_type=jnp.float32)
    lane = lax.broadcasted_iota(jnp.int32, (1, wide), 1)
    weight = weights[0]
    for freq in range(1, freq_count):
        weight = jnp.where(lane // 2 % freq_count == freq, weights[freq], weight)
    cube = (left * weight).reshape(devices, half, wide)
    swapped = jnp.concatenate([cube[:, val_count:], -cube[:, :val_count]], 1)
    left = jnp.where((lane % 2 == 1)[None], swapped, cube).reshape(depth, wide).astype(jnp.bfloat16)
    out_ref[...] = lax.dot_general(
        left, right, (((0,), (0,)), ((), ())), preferred_element_type=jnp.float32
    ).astype(jnp.bfloat16)

    pltpu.make_async_copy(from_line, from_line, line_send).wait()
    for held, sem in ((rows_in, 0), (cols_in, 1)):
        sent = held.at[pl.ds(0, (plane_count - 1) * grow_count)]
        pltpu.make_async_copy(sent, sent, plane_send.at[sem]).wait()


def on_device(sizes, valence, conduction, val_energy, cond_energy, frequencies, gvec_index, first_band):
    band_count, grow_count, gcol_count = sizes
    devices = band_count * grow_count * gcol_count
    val_count = val_energy.shape[0]
    freq_count = frequencies.shape[0]
    num_gvec = gvec_index.shape[0]
    rows = val_count * GRID
    num_tiles = num_gvec // TILE
    col_tiles = num_tiles // gcol_count
    tile_shape = (4 * val_count, LANES)
    operands = (
        valence,
        conduction,
        jnp.asarray(plane_table()),
        jnp.asarray(phase_table(val_count)),
        gvec_index.reshape(num_tiles // 2, 1, WIDE),
        val_energy[None],
        cond_energy[None],
        frequencies[None],
        first_band[None],
    )
    out_shape = (TILE * freq_count * 2, num_gvec // gcol_count)
    out = pl.pallas_call(
        functools.partial(kernel, sizes),
        out_shape=jax.ShapeDtypeStruct(out_shape, jnp.bfloat16),
        in_specs=[pl.BlockSpec(memory_space=pl.ANY)] * len(operands),
        out_specs=pl.BlockSpec(memory_space=pltpu.VMEM),
        scratch_shapes=[
            pltpu.VMEM(valence.shape, jnp.bfloat16),
            pltpu.VMEM(conduction.shape, jnp.bfloat16),
            pltpu.VMEM((CHUNKS, PLANE, WIDE), jnp.bfloat16),
            *(pltpu.VMEM(operand.shape, operand.dtype) for operand in operands[3:]),
            pltpu.VMEM((2 * rows, PLANE), jnp.bfloat16),
            pltpu.VMEM((2 * rows, CHUNKS * CHUNK), jnp.bfloat16),
            pltpu.VMEM((num_tiles,) + tile_shape, jnp.bfloat16),
            pltpu.VMEM((grow_count - 1, num_tiles) + tile_shape, jnp.bfloat16),
            pltpu.VMEM((devices,) + tile_shape, jnp.bfloat16),
            pltpu.VMEM((devices, col_tiles) + tile_shape, jnp.bfloat16),
            pltpu.SemaphoreType.DMA((len(operands) - 1,)),
            pltpu.SemaphoreType.DMA((CHUNKS,)),
            pltpu.SemaphoreType.DMA,
            pltpu.SemaphoreType.DMA((grow_count - 1, num_tiles // 2)),
            pltpu.SemaphoreType.DMA((2,)),
            pltpu.SemaphoreType.DMA((2,)),
        ],
        compiler_params=pltpu.CompilerParams(
            collective_id=0, has_side_effects=True, vmem_limit_bytes=63 * 2**20
        ),
    )(*operands)
    out = out.reshape(TILE, freq_count, 2, num_gvec // gcol_count)
    row_count = num_gvec // (grow_count * band_count)
    if row_count < TILE:
        block = lax.axis_index("grow") * band_count + lax.axis_index("band")
        out = lax.dynamic_slice_in_dim(out, block * row_count % TILE, row_count, 0)
    return out


def solution(mesh):
    sizes = tuple(mesh.shape[name] for name in ("band", "grow", "gcol"))
    return jax.shard_map(
        functools.partial(on_device, sizes),
        mesh=mesh,
        in_specs=(P(), P(("band", "grow", "gcol"), None), P(), P(), P(), P(), P()),
        out_specs=P(("grow", "band"), None, None, "gcol"),
        check_vma=False,
    )
```
